32 devices in a mesh: groups: 2 (over y), tensor: 4 (over z), seq: 2 (over x), kv: 2 (over core).
Axes of the slice: x: 2, y: 2, z: 4, core: 2. Of those that a mesh axis runs over, the one named last changes fastest.
Arguments:
- hidden_rows: bfloat16 [384, 8192], P(('groups', 'tensor', 'seq')), parts along dimension 0, may hold values from -40 to 40
- kv_weight: bfloat16 [2, 8192, 8192], P('kv', 'seq', 'tensor'), may hold values from -0.0625 to 0.0625
- block_lengths: int32 [8], P('groups'), parts along dimension 0, may hold values from 1 to 96, 192 in all
- sign_bits: int32 [8192], replicated, may hold values from 0 to 1
Outputs:
- cache_rows: bfloat16 [2, 384, 8192], P('kv', ('groups', 'tensor', 'seq')), parts along dimension 1
- token_scales: float32 [2, 384], P('kv', ('groups', 'tensor', 'seq')), parts along dimension 1
The draws below stay inside these ranges and needn't reach their ends.
There are 2 independent parts, one for each index of `groups`. The reference program is written for one: setup_inputs(seed, part) draws one part's arguments, and reference() takes and returns one part's arrays. A program takes and returns all parts, laid end to end along the dimension named above; an argument that names none is the same for every part. Nothing has to cross between parts.
Inputs may be any that keep to these rules, and one draw needn't show every extreme that they name: `block_lengths`: the four lengths sum to 192; the largest is exactly 96.
All inputs are finite; a program needn't handle non-finite values. Where the reference program divides by a largest or mean magnitude, that divisor is 1e-20 or more.
Results may differ from the reference program's by a relative error of at most 0.001.
Values may be sent and summed in bfloat16 or wider, within the bound.
No kernel may reach another device: no remote copies, remote signals or barrier semaphores. Data moves between devices by JAX's collectives and lax.ppermute only.
A program may use at most 128 MiB of HBM per device.

```python
import math
import jax
import jax.numpy as jnp
import numpy as np
from jax import lax

D = 8192
HEADS = 64
HEAD = 128
HD = 8192
TOKENS = 192


def draw_hidden_rows(key, part):
    key = jax.random.fold_in(key, 11)
    first, second = jax.random.split(key, 2)
    spread = jnp.exp(jax.random.uniform(second, (TOKENS, 1)) * math.log(10.0))
    base = jax.random.truncated_normal(first, -4.0, 4.0, (TOKENS, D))
    return (base * spread).astype(jnp.bfloat16)


def touch_ends(array, own_key, low, largest):
    dims = array.shape
    index_at = [jax.random.randint(jax.random.fold_in(own_key, axis), (), 0, dims[axis]) for axis in range(len(dims))]
    array = array.at[tuple(index_at)].set(low)
    longest = dims.index(max(dims))
    index_at[longest] = (index_at[longest] + 1) % dims[longest]
    return array.at[tuple(index_at)].set(largest)


def shard_levels(own_key, dims, cuts, smallest, top_value):
    level = 1.0
    for axis_at, parts in cuts:
        draws = jax.random.uniform(jax.random.fold_in(jax.random.fold_in(own_key, 6), axis_at), (parts,), jnp.float32, smallest / len(cuts), top_value / len(cuts))
        level = level * jnp.repeat(jnp.exp(draws), dims[axis_at] // parts).reshape((-1,) + (1,) * (len(dims) - 1 - axis_at))
    return level


def length_profile(count, total, reach, slope):
    weights = [(1 << 20) // math.isqrt(grade ** slope) + 1 for grade in range(2, count + 1)]
    surplus, given = total - reach - (count - 1), [1] * (count - 1)
    while surplus > 0:
        movable = [i for i in range(count - 1) if given[i] < reach]
        whole, budget = sum([weights[i] for i in movable]), surplus
        for i in movable:
            more = min(reach - given[i], max(1, budget * weights[i] // whole), surplus)
            given[i] = given[i] + more
            surplus = surplus - more
    return np.array([reach] + given)


def uneven(stream_key, number_of, total, reach, lean):
    if number_of == 2:
        one = jax.random.randint(stream_key, (), max(1, total - reach), min(reach, total - 1) + 1)
        return jnp.stack([one, total - one])
    sizes = jnp.asarray(length_profile(number_of, total, reach, lean), jnp.int32)
    couples = (number_of - 1) // 2
    donor, sink = sizes[1:1 + 2 * couples:2], sizes[2:2 + 2 * couples:2]
    slack = jnp.minimum(donor - 1, reach - sink)
    moved = jax.random.randint(jax.random.fold_in(stream_key, 1), (couples,), 0, 1 << 20) % (slack + 1)
    sizes = sizes.at[1:1 + 2 * couples:2].set(donor - moved).at[2:2 + 2 * couples:2].set(sink + moved)
    return sizes[jax.random.permutation(jax.random.fold_in(stream_key, 2), number_of)]


def bell_draw(stream_key, extent, scale, limit, cuts=(), kind=jnp.bfloat16):
    gain = shard_levels(stream_key, extent, cuts, -0.22, 0.18) if cuts else 1.0
    values = jax.random.normal(stream_key, extent, jnp.float32) * scale * gain
    return jnp.minimum(jnp.maximum(values, -limit), limit).astype(kind)


def setup_inputs(seed: int = 0, part: int = 0) -> dict:
    keys = jax.random.split(jax.random.key(seed), 5)
    own_keys = jax.random.split(jax.random.fold_in(keys[4], part), 5)
    hidden_rows = draw_hidden_rows(jax.random.fold_in(jax.random.fold_in(keys[4], part), 71), part)
    kv_weight = bell_draw(keys[1], (2, D, HD), D ** -0.5, 0.0625, ((0, 2), (1, 2), (2, 4)))
    block_lengths = uneven(own_keys[2], 4, TOKENS, TOKENS // 2, 1).astype(jnp.int32)
    sign_bits = touch_ends(jax.random.randint(keys[3], (HD,), 0, 2), jax.random.fold_in(keys[3], 1), 0, 1).astype(jnp.int32)
    return {"hidden_rows": hidden_rows, "kv_weight": kv_weight, "block_lengths": block_lengths, "sign_bits": sign_bits}


def sylvester(order):
    index = jnp.arange(order, dtype=jnp.int32)
    both = jnp.bitwise_and(index[:, None], index[None, :])
    parity = jnp.zeros((order, order), jnp.int32)
    for bit in range(order.bit_length() - 1):
        parity = parity + jnp.bitwise_and(jnp.right_shift(both, bit), 1)
    return (1 - 2 * (parity % 2)).astype(jnp.float32) / jnp.sqrt(jnp.float32(order))

def positions(glob, starts):
    glob = glob.astype(jnp.int32)
    hits = glob[:, None] >= starts[None, :]
    start_of = lax.optimization_barrier(jnp.max(jnp.where(hits, starts[None, :], 0), axis=1))
    return (glob - start_of).astype(jnp.float32)

def rotary(feats, place):
    half = HEAD // 2
    freq = jnp.float32(1000000.0) ** (-2.0 * jnp.arange(half, dtype=jnp.float32) / HEAD)
    angle = place[:, None] * freq[None, :]
    cosine = jnp.cos(angle)[:, None, :]
    sine = jnp.sin(angle)[:, None, :]
    first = feats[..., :half]
    second = feats[..., half:]
    return jnp.concatenate([first * cosine - second * sine, second * cosine + first * sine], axis=-1)

def reference(hidden_rows, kv_weight, block_lengths, sign_bits):
    starts = (jnp.cumsum(block_lengths) - block_lengths).astype(jnp.int32)
    place = positions(jnp.arange(TOKENS, dtype=jnp.int32), starts)
    flip = (1 - 2 * sign_bits).astype(jnp.float32).reshape(HEADS, HEAD)
    inner = sylvester(HEAD)
    outer = sylvester(HEADS)
    caches = []
    scales = []
    for which in range(2):
        proj = jnp.dot(hidden_rows, kv_weight[which], preferred_element_type=jnp.float32)
        feats = proj.reshape(TOKENS, HEADS, HEAD)
        if which == 0:
            feats = rotary(feats, place)
        feats = feats * flip
        feats = jnp.einsum('the,ed->thd', feats, inner, precision=lax.Precision.HIGHEST)
        feats = jnp.einsum('the,hg->tge', feats, outer, precision=lax.Precision.HIGHEST)
        feats = feats.reshape(TOKENS, HD)
        top = lax.optimization_barrier(jnp.max(jnp.abs(feats), axis=1))
        caches.append((feats / (top + 1e-06)[:, None]).astype(jnp.bfloat16))
        scales.append(top)
    return (jnp.stack(caches), jnp.stack(scales))
```

```python
import functools

import jax
import jax.numpy as jnp
from jax import lax
from jax.experimental import pallas as pl
from jax.experimental.pallas import tpu as pltpu
from jax.sharding import PartitionSpec as P

HEAD = 128
LANES = 128
FULL = 32000.0
STEPS = 64.0
TINY = 1e-30


def encode(block):
    top = jnp.max(jnp.abs(block), axis=1, keepdims=True)
    code = jnp.ceil(jnp.log2(jnp.maximum(top, TINY)) * STEPS)
    coded = jnp.round(block * (jnp.exp2(code * (-1.0 / STEPS)) * FULL))
    return coded.astype(jnp.int32).astype(jnp.int16), code


def scale_of(codes):
    return jnp.exp2(codes.astype(jnp.int32).astype(jnp.float32) * (1.0 / STEPS)) * (1.0 / FULL)


def decode(coded, scale):
    return coded.astype(jnp.int32).astype(jnp.float32) * scale


def lane_of(rows):
    return lax.broadcasted_iota(jnp.int32, (rows, LANES), 1)


def first_half(at_ref, rows_ref, w_ref, acc_ref):
    acc_ref[...] = jnp.dot(rows_ref[...], w_ref[...], preferred_element_type=jnp.float32)


def second_half(own, tile, at_ref, rows_ref, w_ref, acc_ref, keep_ref, send_ref, codes):
    step = pl.program_id(0)
    columns = keep_ref.shape[1] * pl.num_programs(0)
    total = acc_ref[...] + jnp.dot(rows_ref[...], w_ref[...], preferred_element_type=jnp.float32)
    keep_ref[...] = total[:own]
    away = total.shape[0] - own

    @pl.when(step == 0)
    def _():
        codes[...] = jnp.zeros_like(codes)

    found = codes[...]
    lane = lane_of(away)
    for head in range(tile // HEAD):
        coded, code = encode(total[own:, head * HEAD : (head + 1) * HEAD])
        send_ref[:, pl.ds(pl.multiple_of(step * tile + head * HEAD, HEAD), HEAD)] = coded
        found = jnp.where(lane == step * (tile // HEAD) + head, code, found)
    codes[...] = found

    @pl.when(step == pl.num_programs(0) - 1)
    def _():
        send_ref[:, send_ref.shape[1] - LANES :] = codes[...].astype(jnp.int32).astype(jnp.int16)


def middle(tok_dev, count, *refs):
    keep_ref, got_refs, own_ref, out_refs = refs[0], refs[1 : count], refs[count], refs[count + 1 :]
    heads = keep_ref.shape[1] // HEAD
    columns = heads * HEAD
    rows = keep_ref.shape[0]
    away = rows - tok_dev
    scales = [scale_of(ref[:, columns:]) for ref in got_refs]
    codes = jnp.zeros((away, LANES), jnp.float32)
    lane = lane_of(away)
    for head in range(heads):
        at = pl.ds(head * HEAD, HEAD)
        total = keep_ref[:, at]
        for ref, scale in zip(got_refs, scales):
            total = total + decode(ref[:, at], scale[:, head : head + 1])
        own_ref[:, at] = total[:tok_dev]
        coded, code = encode(total[tok_dev:])
        codes = jnp.where(lane == head, code, codes)
        for k, ref in enumerate(out_refs):
            ref[:, at] = coded[k * tok_dev : (k + 1) * tok_dev]
    codes = codes.astype(jnp.int32).astype(jnp.int16)
    for k, ref in enumerate(out_refs):
        ref[:, columns:] = codes[k * tok_dev : (k + 1) * tok_dev]


def butterflies(blocks):
    blocks = list(blocks)
    span = 1
    while span < len(blocks):
        for i in range(len(blocks)):
            if not i & span:
                a, b = blocks[i], blocks[i + span]
                blocks[i], blocks[i + span] = a + b, a - b
        span *= 2
    return blocks


def final(count, *refs):
    own_ref, got_refs = refs[0], refs[1:count]
    cos_ref, sin_ref, flip_ref, inner_ref, signs_ref, out_ref, top_ref, stage = refs[count:]
    tok = own_ref.shape[0]
    columns = own_ref.shape[1]
    heads = columns // HEAD
    cosine, sine, inner = cos_ref[...], sin_ref[...], inner_ref[...]
    for k in range(count):
        scale = None if k == 0 else scale_of(got_refs[k - 1][:, columns:])
        for head in range(heads):
            at = pl.ds(head * HEAD, HEAD)
            if k == 0:
                block = own_ref[:, at]
            else:
                block = decode(got_refs[k - 1][:, at], scale[:, head : head + 1])
            block = block * cosine + pltpu.roll(block, HEAD // 2, 1) * sine
            block = block * flip_ref[pl.ds(k, 1), at]
            stage[pl.ds((k * heads + head) * tok, tok), :] = block
    whole = stage[...]
    high = whole.astype(jnp.bfloat16)
    rest = whole - high.astype(jnp.float32)
    mid = rest.astype(jnp.bfloat16)
    low = (rest - mid.astype(jnp.float32)).astype(jnp.bfloat16)
    dot = functools.partial(jnp.dot, preferred_element_type=jnp.float32)
    stage[...] = dot(low, inner) + dot(mid, inner) + dot(high, inner)
    norm = 1.0 / float(HEAD * heads * count) ** 0.5
    for k in range(count):
        blocks = [stage[pl.ds((k * heads + head) * tok, tok), :] for head in range(heads)]
        for head, block in enumerate(butterflies(blocks)):
            stage[pl.ds((k * heads + head) * tok, tok), :] = block
    top = jnp.zeros((tok, HEAD), jnp.float32)
    for head in range(heads):
        blocks = [stage[pl.ds((k * heads + head) * tok, tok), :] for k in range(count)]
        for k, block in enumerate(butterflies(blocks)):
            block = block * norm
            stage[pl.ds((k * heads + head) * tok, tok), :] = block
            top = jnp.maximum(top, jnp.abs(block))
    top = jnp.max(top, axis=1, keepdims=True)
    top_ref[...] = jnp.broadcast_to(top, (tok, HEAD))
    inverse = 1.0 / (top + 1e-06)
    for k in range(count):
        factor = inverse * signs_ref[k]
        for head in range(heads):
            block = stage[pl.ds((k * heads + head) * tok, tok), :] * factor
            out_ref[:, pl.ds((k * heads + head) * HEAD, HEAD)] = block.astype(jnp.bfloat16)


def parity_signs(both, bits):
    parity = jnp.zeros_like(both)
    for bit in range(bits):
        parity = parity + jnp.bitwise_and(jnp.right_shift(both, bit), 1)
    return (1 - 2 * (parity % 2)).astype(jnp.float32)


def swap(array, axis, count, offset):
    return lax.ppermute(array, axis, [(i, i ^ offset) for i in range(count)])


def gather(block, count, at):
    if count != 4:
        return [block] + [swap(block, "tensor", count, k) for k in range(1, count)]
    two = swap(block, "tensor", count, 2)
    one = swap(block, "tensor", count, 1)
    near = lax.ppermute(block, "tensor", [(1, 2), (2, 1)])
    far = lax.ppermute(two, "tensor", [(1, 0), (2, 3)])
    inside = jnp.logical_or(at == 1, at == 2)
    return [block, one, two, jnp.where(inside, near, far)]


def per_device(hidden_rows, kv_weight, block_lengths, sign_bits):
    tok_dev, depth = hidden_rows.shape
    rows_dev, columns = kv_weight.shape[1:]
    which, tensor_at, seq_at = (lax.axis_index(name) for name in ("kv", "tensor", "seq"))
    cores, tensors, seqs = (lax.axis_size(name) for name in ("kv", "tensor", "seq"))
    heads = columns // HEAD
    weight = kv_weight[0]
    part = rows_dev // cores
    vmem = pl.BlockSpec(memory_space=pltpu.VMEM)
    big = 48 << 20

    def columns_for(seq):
        return lax.dynamic_slice_in_dim(hidden_rows, (seq * cores + which) * part, part, 1)

    pieces = gather(columns_for(seq_at), tensors, tensor_at)
    for j in range(1, seqs):
        there = jnp.bitwise_xor(seq_at, j)
        pieces += gather(swap(columns_for(there), "seq", seqs, j), tensors, tensor_at)
    mine = jnp.concatenate(pieces, axis=0)
    other = swap(mine, "kv", cores, 1)
    rows = mine.shape[0]
    own = rows // seqs
    tile = min(256, columns)
    steps = columns // tile

    def matmul(kernel, at, given, specs, outs, out_specs, scratch):
        return pl.pallas_call(
            kernel,
            grid_spec=pltpu.PrefetchScalarGridSpec(
                num_scalar_prefetch=1,
                grid=(steps,),
                in_specs=[
                    pl.BlockSpec((rows, part), lambda n, at: (0, 0)),
                    pl.BlockSpec((part, tile), lambda n, at: (at[0], n)),
                ]
                + specs,
                out_specs=out_specs,
                scratch_shapes=scratch,
            ),
            out_shape=outs,
            compiler_params=pltpu.CompilerParams(vmem_limit_bytes=big),
            cost_estimate=pl.CostEstimate(
                flops=2 * rows * part * columns, bytes_accessed=2 * part * columns, transcendentals=0
            ),
        )(at[None], *given)

    strip = pl.BlockSpec((rows, tile), lambda n, at: (0, n))
    acc = matmul(
        first_half, which, (mine, weight), [], jax.ShapeDtypeStruct((rows, columns), jnp.float32), strip, []
    )
    wide = columns + LANES
    keep, send = matmul(
        functools.partial(second_half, own, tile),
        1 - which,
        (other, weight, acc),
        [strip],
        (
            jax.ShapeDtypeStruct((own, columns), jnp.float32),
            jax.ShapeDtypeStruct((rows - own, wide), jnp.int16),
        ),
        (
            pl.BlockSpec((own, tile), lambda n, at: (0, n)),
            pl.BlockSpec((rows - own, wide), lambda n, at: (0, 0)),
        ),
        [pltpu.VMEM((rows - own, LANES), jnp.float32)],
    )
    got = [swap(send[(j - 1) * own : j * own], "seq", seqs, j) for j in range(1, seqs)]
    parts = pl.pallas_call(
        functools.partial(middle, tok_dev, seqs),
        in_specs=[vmem] * seqs,
        out_specs=[vmem] * tensors,
        out_shape=[jax.ShapeDtypeStruct((tok_dev, columns), jnp.float32)]
        + [jax.ShapeDtypeStruct((tok_dev, wide), jnp.int16)] * (tensors - 1),
        compiler_params=pltpu.CompilerParams(vmem_limit_bytes=big),
    )(keep, *got)
    blocks = [parts[0]] + [swap(parts[k], "tensor", tensors, k) for k in range(1, tensors)]

    starts = jnp.cumsum(block_lengths) - block_lengths
    glob = (tensor_at * seqs + seq_at) * tok_dev + jnp.arange(tok_dev, dtype=jnp.int32)
    hits = glob[:, None] >= starts[None, :]
    place = (glob - jnp.max(jnp.where(hits, starts[None, :], 0), axis=1)).astype(jnp.float32)
    half = HEAD // 2
    freq = jnp.float32(1000000.0) ** (-2.0 * jnp.arange(half, dtype=jnp.float32) / HEAD)
    angle = place[:, None] * freq[None, :]
    cosine = jnp.where(which == 0, jnp.cos(angle), 1.0)
    sine = jnp.where(which == 0, jnp.sin(angle), 0.0)
    cosine = jnp.concatenate([cosine, cosine], axis=1)
    sine = jnp.concatenate([-sine, sine], axis=1)
    order = jnp.bitwise_xor(jnp.arange(tensors, dtype=jnp.int32), tensor_at)
    flip = (1 - 2 * sign_bits).astype(jnp.float32).reshape(tensors, columns)[order]
    bits = (tensors - 1).bit_length()
    signs = parity_signs(jnp.bitwise_and(jnp.arange(tensors, dtype=jnp.int32), tensor_at), bits)
    index = jnp.arange(HEAD, dtype=jnp.int32)
    inner = parity_signs(jnp.bitwise_and(index[:, None], index[None, :]), 7).astype(jnp.bfloat16)

    cache, top = pl.pallas_call(
        functools.partial(final, tensors),
        in_specs=[vmem] * (tensors + 4) + [pl.BlockSpec(memory_space=pltpu.SMEM)],
        out_specs=[vmem] * 2,
        out_shape=[
            jax.ShapeDtypeStruct((tok_dev, depth), jnp.bfloat16),
            jax.ShapeDtypeStruct((tok_dev, HEAD), jnp.float32),
        ],
        scratch_shapes=[pltpu.VMEM((tensors * heads * tok_dev, HEAD), jnp.float32)],
        compiler_params=pltpu.CompilerParams(vmem_limit_bytes=big),
    )(*blocks, cosine, sine, flip, inner, signs)
    return (cache[None], top[:, 0][None])


def solution(mesh):
    return jax.shard_map(
        per_device,
        mesh=mesh,
        in_specs=(P(("groups", "tensor", "seq"), None), P("kv", "seq", "tensor"), P("groups"), P()),
        out_specs=(
            P("kv", ("groups", "tensor", "seq"), None),
            P("kv", ("groups", "tensor", "seq")),
        ),
        check_vma=False,
    )
```

```python
import functools

import jax
import jax.numpy as jnp
from jax import lax
from jax.experimental import pallas as pl
from jax.experimental.pallas import tpu as pltpu
from jax.sharding import PartitionSpec as P

HEAD = 128
LANES = 128
FULL = 32000.0
STEPS = 64.0
TINY = 1e-30


def encode(block):
    top = jnp.max(jnp.abs(block), axis=1, keepdims=True)
    code = jnp.ceil(jnp.log2(jnp.maximum(top, TINY)) * STEPS)
    coded = jnp.round(block * (jnp.exp2(code * (-1.0 / STEPS)) * FULL))
    return coded.astype(jnp.int32).astype(jnp.int16), code


def scale_of(codes):
    return jnp.exp2(codes.astype(jnp.int32).astype(jnp.float32) * (1.0 / STEPS)) * (1.0 / FULL)


def decode(coded, scale):
    return coded.astype(jnp.int32).astype(jnp.float32) * scale


def lane_of(rows):
    return lax.broadcasted_iota(jnp.int32, (rows, LANES), 1)


def load(offset, pieces, w_ref, out_ref, sems):
    rows = out_ref.shape[0]
    index = lax.rem(lax.axis_index("kv") + offset, lax.axis_size("kv"))
    piece = rows // pieces
    copies = []
    for i in range(pieces):
        start = pl.multiple_of(index * rows + i * piece, piece)
        copies.append(
            pltpu.make_async_copy(w_ref.at[pl.ds(start, piece)], out_ref.at[pl.ds(i * piece, piece)], sems.at[i])
        )
    for copy in copies:
        copy.start()
    for copy in copies:
        copy.wait()


def first_half(tile, rows_ref, w_ref, acc_ref):
    for first in range(0, acc_ref.shape[1], tile):
        at = slice(first, first + tile)
        acc_ref[:, at] = jnp.dot(rows_ref[...], w_ref[:, at], preferred_element_type=jnp.float32)


def second_half(begin, tile, rows_ref, w_ref, acc_ref, keep_ref, send_ref):
    own, width = keep_ref.shape
    away = send_ref.shape[0]
    codes = jnp.zeros((away, LANES), jnp.float32)
    lane = lane_of(away)
    for first in range(0, width, tile):
        at = slice(begin + first, begin + first + tile)
        total = acc_ref[:, at] + jnp.dot(rows_ref[...], w_ref[:, at], preferred_element_type=jnp.float32)
        keep_ref[:, first : first + tile] = total[:own]
        for head in range(tile // HEAD):
            coded, code = encode(total[own:, head * HEAD : (head + 1) * HEAD])
            send_ref[:, first + head * HEAD : first + (head + 1) * HEAD] = coded
            codes = jnp.where(lane == first // HEAD + head, code, codes)
    send_ref[:, width:] = codes.astype(jnp.int32).astype(jnp.int16)


def middle(tok_dev, count, *refs):
    keep_ref, got_refs, own_ref, out_refs = refs[0], refs[1 : count], refs[count], refs[count + 1 :]
    heads = keep_ref.shape[1] // HEAD
    columns = heads * HEAD
    rows = keep_ref.shape[0]
    away = rows - tok_dev
    scales = [scale_of(ref[:, columns:]) for ref in got_refs]
    codes = jnp.zeros((away, LANES), jnp.float32)
    lane = lane_of(away)
    for head in range(heads):
        at = pl.ds(head * HEAD, HEAD)
        total = keep_ref[:, at]
        for ref, scale in zip(got_refs, scales):
            total = total + decode(ref[:, at], scale[:, head : head + 1])
        own_ref[:, at] = total[:tok_dev]
        coded, code = encode(total[tok_dev:])
        codes = jnp.where(lane == head, code, codes)
        for k, ref in enumerate(out_refs):
            ref[:, at] = coded[k * tok_dev : (k + 1) * tok_dev]
    codes = codes.astype(jnp.int32).astype(jnp.int16)
    for k, ref in enumerate(out_refs):
        ref[:, columns:] = codes[k * tok_dev : (k + 1) * tok_dev]


def butterflies(blocks):
    blocks = list(blocks)
    span = 1
    while span < len(blocks):
        for i in range(len(blocks)):
            if not i & span:
                a, b = blocks[i], blocks[i + span]
                blocks[i], blocks[i + span] = a + b, a - b
        span *= 2
    return blocks


def parity_signs(both, bits):
    parity = jnp.zeros_like(both)
    for bit in range(bits):
        parity = parity + jnp.bitwise_and(jnp.right_shift(both, bit), 1)
    return (1 - 2 * jnp.bitwise_and(parity, 1)).astype(jnp.float32)


def final(count, chunks, *refs):
    block_refs = refs[: count * chunks]
    cos_ref, sin_ref, bits_ref, out_ref, top_ref, stage = refs[count * chunks :]
    tok, width = block_refs[0].shape
    per_chunk = width // HEAD
    heads = per_chunk * chunks
    columns = heads * HEAD
    bits = (count - 1).bit_length()
    tensor_at = lax.axis_index("tensor")
    cosine, sine = cos_ref[...], sin_ref[...]
    both = lax.broadcasted_iota(jnp.int32, (HEAD, HEAD), 0) & lax.broadcasted_iota(jnp.int32, (HEAD, HEAD), 1)
    inner = parity_signs(both, 7).astype(jnp.bfloat16)
    for k in range(count):
        there = pl.multiple_of(jnp.bitwise_xor(tensor_at, k) * columns, HEAD)
        flip = (1 - 2 * bits_ref[:, pl.ds(there, columns)]).astype(jnp.float32)
        for chunk in range(chunks):
            ref = block_refs[chunk * count + k]
            scale = None if k == 0 else scale_of(ref[:, width:])
            for head in range(per_chunk):
                block = ref[:, head * HEAD : (head + 1) * HEAD]
                if k:
                    block = decode(block, scale[:, head : head + 1])
                at = chunk * per_chunk + head
                block = block * cosine + pltpu.roll(block, HEAD // 2, 1) * sine
                block = block * flip[:, at * HEAD : (at + 1) * HEAD]
                stage[pl.ds((k * heads + at) * tok, tok), :] = block
    whole = stage[...]
    high = whole.astype(jnp.bfloat16)
    rest = whole - high.astype(jnp.float32)
    mid = rest.astype(jnp.bfloat16)
    low = (rest - mid.astype(jnp.float32)).astype(jnp.bfloat16)
    dot = functools.partial(jnp.dot, preferred_element_type=jnp.float32)
    stage[...] = dot(low, inner) + dot(mid, inner) + dot(high, inner)
    norm = 1.0 / float(HEAD * heads * count) ** 0.5
    for k in range(count):
        blocks = [stage[pl.ds((k * heads + head) * tok, tok), :] for head in range(heads)]
        for head, block in enumerate(butterflies(blocks)):
            stage[pl.ds((k * heads + head) * tok, tok), :] = block
    top = jnp.zeros((tok, HEAD), jnp.float32)
    for head in range(heads):
        blocks = [stage[pl.ds((k * heads + head) * tok, tok), :] for k in range(count)]
        for k, block in enumerate(butterflies(blocks)):
            block = block * norm
            stage[pl.ds((k * heads + head) * tok, tok), :] = block
            top = jnp.maximum(top, jnp.abs(block))
    top = jnp.max(top, axis=1, keepdims=True)
    row = lax.broadcasted_iota(jnp.int32, (tok, HEAD), 0)
    line = jnp.sum(jnp.where(row == lane_of(tok), top, 0.0), axis=0, keepdims=True)
    top_ref[...] = line[:, :tok]
    inverse = 1.0 / (top + 1e-06)
    for k in range(count):
        factor = inverse * parity_signs(jnp.bitwise_and(tensor_at, k), bits)
        for head in range(heads):
            block = stage[pl.ds((k * heads + head) * tok, tok), :] * factor
            out_ref[:, pl.ds((k * heads + head) * HEAD, HEAD)] = block.astype(jnp.bfloat16)


def swap(array, axis, count, offset):
    return lax.ppermute(array, axis, [(i, i ^ offset) for i in range(count)])


def gather(own, others, count):
    if count != 4:
        pieces = []
        for block in [own] + others:
            pieces += [block] + [swap(block, "tensor", count, k) for k in range(1, count)]
        return jnp.concatenate(pieces, axis=0)
    tok = own.shape[0]
    mine = jnp.concatenate([own] + others, axis=0)
    two = [swap(own, "tensor", count, 2), swap(mine[tok:], "tensor", count, 2)]
    two = jnp.concatenate(two, axis=0)
    one = swap(mine, "tensor", count, 1)
    near = lax.ppermute(mine, "tensor", [(1, 2), (2, 1)])
    far = lax.ppermute(two, "tensor", [(1, 0), (2, 3)])
    blocks = jnp.stack([mine, one, two, near + far])
    blocks = blocks.reshape(count, 1 + len(others), tok, own.shape[1])
    return jnp.swapaxes(blocks, 0, 1).reshape(-1, own.shape[1])


def per_device(hidden_rows, kv_weight, block_lengths, sign_bits):
    tok_dev, depth = hidden_rows.shape
    rows_dev, columns = kv_weight.shape[1:]
    which, tensor_at, seq_at = (lax.axis_index(name) for name in ("kv", "tensor", "seq"))
    cores, tensors, seqs = (lax.axis_size(name) for name in ("kv", "tensor", "seq"))
    weight = kv_weight[0]
    part = rows_dev // cores
    vmem = pl.BlockSpec(memory_space=pltpu.VMEM)
    chunks = 2 if columns >= 1024 else 1
    width = columns // chunks
    heads = columns // HEAD

    def local(kernel, outs, in_specs, limit, scratch=(), flops=0, moved=0):
        return pl.pallas_call(
            kernel,
            in_specs=in_specs,
            out_specs=jax.tree.map(lambda _: vmem, outs),
            out_shape=outs,
            scratch_shapes=scratch,
            compiler_params=pltpu.CompilerParams(vmem_limit_bytes=limit << 20),
            cost_estimate=pl.CostEstimate(flops=flops, bytes_accessed=moved, transcendentals=0),
        )

    index = jnp.arange(block_lengths.shape[0], dtype=jnp.int32)
    starts = jnp.sum(jnp.where(index[:, None] < index[None, :], block_lengths[:, None], 0), axis=0)
    glob = (tensor_at * seqs + seq_at) * tok_dev + jnp.arange(tok_dev, dtype=jnp.int32)
    hits = glob[:, None] >= starts[None, :]
    place = (glob - jnp.max(jnp.where(hits, starts[None, :], 0), axis=1)).astype(jnp.float32)
    freq = jnp.float32(1000000.0) ** (-2.0 * jnp.arange(HEAD // 2, dtype=jnp.float32) / HEAD)
    angle = place[:, None] * freq[None, :]
    cosine = jnp.where(which == 0, jnp.cos(angle), 1.0)
    sine = jnp.where(which == 0, jnp.sin(angle), 0.0)
    cosine = jnp.concatenate([cosine, cosine], axis=1)
    sine = jnp.concatenate([-sine, sine], axis=1)
    weight, cosine, sine = lax.optimization_barrier((weight, cosine, sine))

    halves = [
        local(
            functools.partial(load, offset, 8),
            pltpu.VMEM((part, columns), weight.dtype),
            [pl.BlockSpec(memory_space=pltpu.HBM)],
            4,
            [pltpu.SemaphoreType.DMA((8,))],
            moved=4 * part * columns,
        )(pltpu.with_memory_space_constraint(weight, pltpu.HBM))
        for offset in range(cores)
    ]

    def columns_for(seq):
        return lax.dynamic_slice_in_dim(hidden_rows, (seq * cores + which) * part, part, 1)

    others = [swap(columns_for(jnp.bitwise_xor(seq_at, j)), "seq", seqs, j) for j in range(1, seqs)]
    mine = gather(columns_for(seq_at), others, tensors)
    mine, *halves = lax.optimization_barrier((mine, *halves))
    other = swap(mine, "kv", cores, 1)
    rows = mine.shape[0]
    own = rows // seqs
    tile = min(256, width)
    limit = 8 if rows < 1024 else 24
    wide = width + LANES
    acc = local(
        functools.partial(first_half, tile),
        jax.ShapeDtypeStruct((rows, columns), jnp.float32),
        [vmem, vmem],
        limit,
        flops=2 * rows * part * columns,
        moved=4 * rows * columns,
    )(mine, pltpu.with_memory_space_constraint(halves[0], pltpu.VMEM))
    blocks = []
    for chunk in range(chunks):
        keep, send = local(
            functools.partial(second_half, chunk * width, tile),
            [
                jax.ShapeDtypeStruct((own, width), jnp.float32),
                jax.ShapeDtypeStruct((rows - own, wide), jnp.int16),
            ],
            [vmem, vmem, vmem],
            limit,
            flops=2 * rows * part * width,
            moved=8 * rows * width,
        )(other, pltpu.with_memory_space_constraint(halves[1], pltpu.VMEM), acc)
        got = [swap(send[(j - 1) * own : j * own], "seq", seqs, j) for j in range(1, seqs)]
        parts = local(
            functools.partial(middle, tok_dev, seqs),
            [jax.ShapeDtypeStruct((tok_dev, width), jnp.float32)]
            + [jax.ShapeDtypeStruct((tok_dev, wide), jnp.int16)] * (tensors - 1),
            [vmem] * seqs,
            limit,
            moved=8 * own * width,
        )(keep, *got)
        blocks += [parts[0]] + [swap(parts[k], "tensor", tensors, k) for k in range(1, tensors)]

    cache, top = local(
        functools.partial(final, tensors, chunks),
        [
            jax.ShapeDtypeStruct((tok_dev, depth), jnp.bfloat16),
            jax.ShapeDtypeStruct((1, tok_dev), jnp.float32),
        ],
        [vmem] * (tensors * chunks + 3),
        32,
        [pltpu.VMEM((tensors * heads * tok_dev, HEAD), jnp.float32)],
    )(*blocks, cosine, sine, sign_bits[None])
    return (cache[None], top)


def solution(mesh):
    return jax.shard_map(
        per_device,
        mesh=mesh,
        in_specs=(P(("groups", "tensor", "seq"), None), P("kv", "seq", "tensor"), P("groups"), P()),
        out_specs=(
            P("kv", ("groups", "tensor", "seq"), None),
            P("kv", ("groups", "tensor", "seq")),
        ),
        check_vma=False,
    )
```

```python
import functools

import jax
import jax.numpy as jnp
from jax import lax
from jax.experimental import pallas as pl
from jax.experimental.pallas import tpu as pltpu
from jax.sharding import PartitionSpec as P

HEAD = 128
LANES = 128
FULL = 32000.0
STEPS = 64.0
TINY = 1e-30


def encode(block):
    top = jnp.max(jnp.abs(block), axis=1, keepdims=True)
    code = jnp.ceil(jnp.log2(jnp.maximum(top, TINY)) * STEPS)
    coded = jnp.round(block * (jnp.exp2(code * (-1.0 / STEPS)) * FULL))
    return coded.astype(jnp.int32).astype(jnp.int16), code


def scale_of(codes):
    return jnp.exp2(codes.astype(jnp.int32).astype(jnp.float32) * (1.0 / STEPS)) * (1.0 / FULL)


def decode(coded, scale):
    return coded.astype(jnp.int32).astype(jnp.float32) * scale


def lane_of(rows):
    return lax.broadcasted_iota(jnp.int32, (rows, LANES), 1)


def load(offset, pieces, w_ref, out_ref, sems):
    rows = out_ref.shape[0]
    index = lax.rem(lax.axis_index("kv") + offset, lax.axis_size("kv"))
    piece = rows // pieces
    copies = []
    for i in range(pieces):
        start = pl.multiple_of(index * rows + i * piece, piece)
        copies.append(
            pltpu.make_async_copy(w_ref.at[pl.ds(start, piece)], out_ref.at[pl.ds(i * piece, piece)], sems.at[i])
        )
    for copy in copies:
        copy.start()
    for copy in copies:
        copy.wait()


def take(rows_ref, *refs):
    out_refs, sems = refs[:-1], refs[-1]
    part = out_refs[0].shape[1]
    copies = []
    for j, out_ref in enumerate(out_refs):
        index = jnp.bitwise_xor(lax.axis_index("seq"), j) * lax.axis_size("kv") + lax.axis_index("kv")
        at = pl.ds(pl.multiple_of(index * part, part), part)
        copies.append(pltpu.make_async_copy(rows_ref.at[:, at], out_ref, sems.at[j]))
    for copy in copies:
        copy.start()
    for copy in copies:
        copy.wait()


def first_half(tile, rows_ref, w_ref, acc_ref):
    for first in range(0, acc_ref.shape[1], tile):
        at = slice(first, first + tile)
        acc_ref[:, at] = jnp.dot(rows_ref[...], w_ref[:, at], preferred_element_type=jnp.float32)


def second_half(begin, tile, rows_ref, w_ref, acc_ref, keep_ref, send_ref):
    own, width = keep_ref.shape
    away = send_ref.shape[0]
    codes = jnp.zeros((away, LANES), jnp.float32)
    lane = lane_of(away)
    for first in range(0, width, tile):
        at = slice(begin + first, begin + first + tile)
        total = acc_ref[:, at] + jnp.dot(rows_ref[...], w_ref[:, at], preferred_element_type=jnp.float32)
        keep_ref[:, first : first + tile] = total[:own]
        for head in range(tile // HEAD):
            coded, code = encode(total[own:, head * HEAD : (head + 1) * HEAD])
            send_ref[:, first + head * HEAD : first + (head + 1) * HEAD] = coded
            codes = jnp.where(lane == first // HEAD + head, code, codes)
    send_ref[:, width:] = codes.astype(jnp.int32).astype(jnp.int16)


def middle(tok_dev, count, *refs):
    keep_ref, got_refs, own_ref, out_refs = refs[0], refs[1 : count], refs[count], refs[count + 1 :]
    heads = keep_ref.shape[1] // HEAD
    columns = heads * HEAD
    rows = keep_ref.shape[0]
    away = rows - tok_dev
    scales = [scale_of(ref[:, columns:]) for ref in got_refs]
    codes = jnp.zeros((away, LANES), jnp.float32)
    lane = lane_of(away)
    for head in range(heads):
        at = pl.ds(head * HEAD, HEAD)
        total = keep_ref[:, at]
        for ref, scale in zip(got_refs, scales):
            total = total + decode(ref[:, at], scale[:, head : head + 1])
        own_ref[:, at] = total[:tok_dev]
        coded, code = encode(total[tok_dev:])
        codes = jnp.where(lane == head, code, codes)
        for k, ref in enumerate(out_refs):
            ref[:, at] = coded[k * tok_dev : (k + 1) * tok_dev]
    codes = codes.astype(jnp.int32).astype(jnp.int16)
    for k, ref in enumerate(out_refs):
        ref[:, columns:] = codes[k * tok_dev : (k + 1) * tok_dev]


def butterflies(blocks):
    blocks = list(blocks)
    span = 1
    while span < len(blocks):
        for i in range(len(blocks)):
            if not i & span:
                a, b = blocks[i], blocks[i + span]
                blocks[i], blocks[i + span] = a + b, a - b
        span *= 2
    return blocks


def parity_signs(both, bits):
    parity = jnp.zeros_like(both)
    for bit in range(bits):
        parity = parity + jnp.bitwise_and(jnp.right_shift(both, bit), 1)
    return (1 - 2 * jnp.bitwise_and(parity, 1)).astype(jnp.float32)


def final(count, chunks, *refs):
    block_refs = refs[: count * chunks]
    cos_ref, sin_ref, bits_ref, out_ref, top_ref, stage = refs[count * chunks :]
    tok, width = block_refs[0].shape
    per_chunk = width // HEAD
    heads = per_chunk * chunks
    columns = heads * HEAD
    bits = (count - 1).bit_length()
    tensor_at = lax.axis_index("tensor")
    cosine, sine = cos_ref[...], sin_ref[...]
    both = lax.broadcasted_iota(jnp.int32, (HEAD, HEAD), 0) & lax.broadcasted_iota(jnp.int32, (HEAD, HEAD), 1)
    inner = parity_signs(both, 7).astype(jnp.bfloat16)
    for k in range(count):
        there = pl.multiple_of(jnp.bitwise_xor(tensor_at, k) * columns, HEAD)
        flip = (1 - 2 * bits_ref[:, pl.ds(there, columns)]).astype(jnp.float32)
        for chunk in range(chunks):
            ref = block_refs[chunk * count + k]
            scale = None if k == 0 else scale_of(ref[:, width:])
            for head in range(per_chunk):
                block = ref[:, head * HEAD : (head + 1) * HEAD]
                if k:
                    block = decode(block, scale[:, head : head + 1])
                at = chunk * per_chunk + head
                block = block * cosine + pltpu.roll(block, HEAD // 2, 1) * sine
                block = block * flip[:, at * HEAD : (at + 1) * HEAD]
                stage[pl.ds((k * heads + at) * tok, tok), :] = block
    whole = stage[...]
    high = whole.astype(jnp.bfloat16)
    rest = whole - high.astype(jnp.float32)
    mid = rest.astype(jnp.bfloat16)
    low = (rest - mid.astype(jnp.float32)).astype(jnp.bfloat16)
    dot = functools.partial(jnp.dot, preferred_element_type=jnp.float32)
    stage[...] = dot(low, inner) + dot(mid, inner) + dot(high, inner)
    norm = 1.0 / float(HEAD * heads * count) ** 0.5
    for k in range(count):
        blocks = [stage[pl.ds((k * heads + head) * tok, tok), :] for head in range(heads)]
        for head, block in enumerate(butterflies(blocks)):
            stage[pl.ds((k * heads + head) * tok, tok), :] = block
    top = jnp.zeros((tok, HEAD), jnp.float32)
    for head in range(heads):
        blocks = [stage[pl.ds((k * heads + head) * tok, tok), :] for k in range(count)]
        for k, block in enumerate(butterflies(blocks)):
            block = block * norm
            stage[pl.ds((k * heads + head) * tok, tok), :] = block
            top = jnp.maximum(top, jnp.abs(block))
    top = jnp.max(top, axis=1, keepdims=True)
    row = lax.broadcasted_iota(jnp.int32, (tok, HEAD), 0)
    line = jnp.sum(jnp.where(row == lane_of(tok), top, 0.0), axis=0, keepdims=True)
    top_ref[...] = line[:, :tok]
    inverse = 1.0 / (top + 1e-06)
    for k in range(count):
        factor = inverse * parity_signs(jnp.bitwise_and(tensor_at, k), bits)
        for head in range(heads):
            block = stage[pl.ds((k * heads + head) * tok, tok), :] * factor
            out_ref[:, pl.ds((k * heads + head) * HEAD, HEAD)] = block.astype(jnp.bfloat16)


def swap(array, axis, count, offset):
    return lax.ppermute(array, axis, [(i, i ^ offset) for i in range(count)])


def gather(own, others, half, count):
    if count != 4:
        pieces = []
        for block in [own] + others:
            pieces += [block] + [swap(block, "tensor", count, k) for k in range(1, count)]
        return jnp.concatenate(pieces, axis=0), half
    tok = own.shape[0]
    mine = jnp.concatenate([own] + others, axis=0)
    two = [swap(own, "tensor", count, 2), swap(mine[tok:], "tensor", count, 2)]
    two = jnp.concatenate(two, axis=0)
    one = swap(mine, "tensor", count, 1)
    mine, one, two, half = lax.optimization_barrier((mine, one, two, half))
    near = lax.ppermute(mine, "tensor", [(1, 2), (2, 1)])
    far = lax.ppermute(two, "tensor", [(1, 0), (2, 3)])
    blocks = jnp.stack([mine, one, two, near + far])
    blocks = blocks.reshape(count, 1 + len(others), tok, own.shape[1])
    return jnp.swapaxes(blocks, 0, 1).reshape(-1, own.shape[1]), half


def per_device(hidden_rows, kv_weight, block_lengths, sign_bits):
    tok_dev, depth = hidden_rows.shape
    rows_dev, columns = kv_weight.shape[1:]
    which, tensor_at, seq_at = (lax.axis_index(name) for name in ("kv", "tensor", "seq"))
    cores, tensors, seqs = (lax.axis_size(name) for name in ("kv", "tensor", "seq"))
    weight = kv_weight[0]
    part = rows_dev // cores
    vmem = pl.BlockSpec(memory_space=pltpu.VMEM)
    chunks = 2 if columns >= 1024 else 1
    width = columns // chunks
    heads = columns // HEAD

    def local(kernel, outs, in_specs, limit, scratch=(), flops=0, moved=0):
        return pl.pallas_call(
            kernel,
            in_specs=in_specs,
            out_specs=jax.tree.map(lambda _: vmem, outs),
            out_shape=outs,
            scratch_shapes=scratch,
            compiler_params=pltpu.CompilerParams(vmem_limit_bytes=limit << 20),
            cost_estimate=pl.CostEstimate(flops=flops, bytes_accessed=moved, transcendentals=0),
        )

    index = jnp.arange(block_lengths.shape[0], dtype=jnp.int32)
    starts = jnp.sum(jnp.where(index[:, None] < index[None, :], block_lengths[:, None], 0), axis=0)
    glob = (tensor_at * seqs + seq_at) * tok_dev + jnp.arange(tok_dev, dtype=jnp.int32)
    hits = glob[:, None] >= starts[None, :]
    place = (glob - jnp.max(jnp.where(hits, starts[None, :], 0), axis=1)).astype(jnp.float32)
    freq = jnp.float32(1000000.0) ** (-2.0 * jnp.arange(HEAD // 2, dtype=jnp.float32) / HEAD)
    angle = place[:, None] * freq[None, :]
    cosine = jnp.where(which == 0, jnp.cos(angle), 1.0)
    sine = jnp.where(which == 0, jnp.sin(angle), 0.0)
    cosine = jnp.concatenate([cosine, cosine], axis=1)
    sine = jnp.concatenate([-sine, sine], axis=1)
    weight, cosine, sine = lax.optimization_barrier((weight, cosine, sine))

    slices = local(
        take,
        [pltpu.VMEM((tok_dev, part), hidden_rows.dtype)] * seqs,
        [pl.BlockSpec(memory_space=pltpu.HBM)],
        4,
        [pltpu.SemaphoreType.DMA((seqs,))],
    )(pltpu.with_memory_space_constraint(hidden_rows, pltpu.HBM))
    others = [swap(slices[j], "seq", seqs, j) for j in range(1, seqs)]
    weight = pltpu.with_memory_space_constraint(weight, pltpu.HBM)
    weight, *others = lax.optimization_barrier((weight, *others))
    halves = [
        local(
            functools.partial(load, offset, 8),
            pltpu.VMEM((part, columns), weight.dtype),
            [pl.BlockSpec(memory_space=pltpu.HBM)],
            4,
            [pltpu.SemaphoreType.DMA((8,))],
            moved=4 * part * columns,
        )(weight)
        for offset in range(cores)
    ]
    mine, halves[0] = gather(slices[0], others, halves[0], tensors)
    mine, *halves = lax.optimization_barrier((mine, *halves))
    other = swap(mine, "kv", cores, 1)
    rows = mine.shape[0]
    own = rows // seqs
    tile = min(256, width)
    limit = 8 if rows < 1024 else 24
    wide = width + LANES
    acc = local(
        functools.partial(first_half, tile),
        jax.ShapeDtypeStruct((rows, columns), jnp.float32),
        [vmem, vmem],
        limit,
        flops=2 * rows * part * columns,
        moved=4 * rows * columns,
    )(mine, pltpu.with_memory_space_constraint(halves[0], pltpu.VMEM))
    blocks = []
    for chunk in range(chunks):
        keep, send = local(
            functools.partial(second_half, chunk * width, tile),
            [
                jax.ShapeDtypeStruct((own, width), jnp.float32),
                jax.ShapeDtypeStruct((rows - own, wide), jnp.int16),
            ],
            [vmem, vmem, vmem],
            limit,
            flops=2 * rows * part * width,
            moved=8 * rows * width,
        )(other, pltpu.with_memory_space_constraint(halves[1], pltpu.VMEM), acc)
        if blocks:
            send, *got = lax.optimization_barrier((send, *got))
        got = [swap(send[(j - 1) * own : j * own], "seq", seqs, j) for j in range(1, seqs)]
        parts = local(
            functools.partial(middle, tok_dev, seqs),
            [jax.ShapeDtypeStruct((tok_dev, width), jnp.float32)]
            + [jax.ShapeDtypeStruct((tok_dev, wide), jnp.int16)] * (tensors - 1),
            [vmem] * seqs,
            limit,
            moved=8 * own * width,
        )(keep, *got)
        blocks += [parts[0]] + [swap(parts[k], "tensor", tensors, k) for k in range(1, tensors)]

    cache, top = local(
        functools.partial(final, tensors, chunks),
        [
            jax.ShapeDtypeStruct((tok_dev, depth), jnp.bfloat16),
            jax.ShapeDtypeStruct((1, tok_dev), jnp.float32),
        ],
        [vmem] * (tensors * chunks + 3),
        32,
        [pltpu.VMEM((tensors * heads * tok_dev, HEAD), jnp.float32)],
    )(*blocks, cosine, sine, sign_bits[None])
    return (cache[None], top)


def solution(mesh):
    return jax.shard_map(
        per_device,
        mesh=mesh,
        in_specs=(P(("groups", "tensor", "seq"), None), P("kv", "seq", "tensor"), P("groups"), P()),
        out_specs=(
            P("kv", ("groups", "tensor", "seq"), None),
            P("kv", ("groups", "tensor", "seq")),
        ),
        check_vma=False,
    )
```

```python
import functools

import jax
import jax.numpy as jnp
from jax import lax
from jax.experimental import pallas as pl
from jax.experimental.pallas import tpu as pltpu
from jax.sharding import PartitionSpec as P

HEAD = 128
LANES = 128
FULL = 32000.0
STEPS = 64.0
TINY = 1e-30


def encode(block):
    top = jnp.max(jnp.abs(block), axis=1, keepdims=True)
    code = jnp.ceil(jnp.log2(jnp.maximum(top, TINY)) * STEPS)
    coded = jnp.round(block * (jnp.exp2(code * (-1.0 / STEPS)) * FULL))
    return coded.astype(jnp.int32).astype(jnp.int16), code


def scale_of(codes):
    return jnp.exp2(codes.astype(jnp.int32).astype(jnp.float32) * (1.0 / STEPS)) * (1.0 / FULL)


def decode(coded, scale):
    return coded.astype(jnp.int32).astype(jnp.float32) * scale


def lane_of(rows):
    return lax.broadcasted_iota(jnp.int32, (rows, LANES), 1)


def load(offset, piece, copies, w_ref, out_ref, sems):
    rows = out_ref.shape[0]
    cores = lax.axis_size("kv")
    index = lax.rem(lax.axis_index("kv") + offset, cores)
    base = index * (w_ref.shape[0] // cores) + piece * rows
    step = rows // copies
    started = []
    for i in range(copies):
        start = pl.multiple_of(base + i * step, step)
        started.append(
            pltpu.make_async_copy(w_ref.at[pl.ds(start, step)], out_ref.at[pl.ds(i * step, step)], sems.at[i])
        )
    for copy in started:
        copy.start()
    for copy in started:
        copy.wait()


def take(rows_ref, *refs):
    out_refs, sems = refs[:-1], refs[-1]
    part = out_refs[0].shape[1]
    copies = []
    for j, out_ref in enumerate(out_refs):
        index = jnp.bitwise_xor(lax.axis_index("seq"), j) * lax.axis_size("kv") + lax.axis_index("kv")
        at = pl.ds(pl.multiple_of(index * part, part), part)
        copies.append(pltpu.make_async_copy(rows_ref.at[:, at], out_ref, sems.at[j]))
    for copy in copies:
        copy.start()
    for copy in copies:
        copy.wait()


def first_half(tile, rows_ref, w_ref, acc_ref):
    for first in range(0, acc_ref.shape[1], tile):
        at = slice(first, first + tile)
        acc_ref[:, at] = jnp.dot(rows_ref[...], w_ref[:, at], preferred_element_type=jnp.float32)


def second_half(row, rows, column, tile, rows_ref, w_ref, acc_ref, keep_ref, *send_refs):
    kept, width = keep_ref.shape
    size = send_refs[0].shape[0]
    codes = jnp.zeros((rows - kept, LANES), jnp.float32)
    lane = lane_of(rows - kept)
    for first in range(0, width, tile):
        at = slice(column + first, column + first + tile)
        total = acc_ref[row : row + rows, at]
        total = total + jnp.dot(rows_ref[row : row + rows, :], w_ref[:, at], preferred_element_type=jnp.float32)
        keep_ref[:, first : first + tile] = total[:kept]
        for begin in range(0, tile, HEAD):
            coded, code = encode(total[kept:, begin : begin + HEAD])
            head = (first + begin) // HEAD
            for i, ref in enumerate(send_refs):
                ref[:, head * HEAD : (head + 1) * HEAD] = coded[i * size : (i + 1) * size]
            codes = jnp.where(lane == head, code, codes)
    codes = codes.astype(jnp.int32).astype(jnp.int16)
    for i, ref in enumerate(send_refs):
        ref[:, width:] = codes[i * size : (i + 1) * size]


def middle(seqs, keep_ref, *refs):
    got_refs, out_refs = refs[: seqs - 1], refs[seqs - 1 :]
    rows, columns = keep_ref.shape
    tok = out_refs[0].shape[0]
    scales = [scale_of(ref[:, columns:]) for ref in got_refs]
    codes = jnp.zeros((rows, LANES), jnp.float32)
    lane = lane_of(rows)
    for head in range(columns // HEAD):
        at = slice(head * HEAD, (head + 1) * HEAD)
        total = keep_ref[:, at]
        for ref, scale in zip(got_refs, scales):
            total = total + decode(ref[:, at], scale[:, head : head + 1])
        coded, code = encode(total)
        codes = jnp.where(lane == head, code, codes)
        for k, ref in enumerate(out_refs):
            ref[:, at] = coded[k * tok : (k + 1) * tok]
    codes = codes.astype(jnp.int32).astype(jnp.int16)
    for k, ref in enumerate(out_refs):
        ref[:, columns:] = codes[k * tok : (k + 1) * tok]


def butterflies(blocks):
    blocks = list(blocks)
    span = 1
    while span < len(blocks):
        for i in range(len(blocks)):
            if not i & span:
                a, b = blocks[i], blocks[i + span]
                blocks[i], blocks[i + span] = a + b, a - b
        span *= 2
    return blocks


def parity_signs(both, bits):
    parity = jnp.zeros_like(both)
    for bit in range(bits):
        parity = parity + jnp.bitwise_and(jnp.right_shift(both, bit), 1)
    return (1 - 2 * jnp.bitwise_and(parity, 1)).astype(jnp.float32)


def local_part(first, chunks, groups, tok, cos_ref, sin_ref, bits_ref, stage):
    cosine, sine = cos_ref[...], sin_ref[...]
    both = lax.broadcasted_iota(jnp.int32, (HEAD, HEAD), 0) & lax.broadcasted_iota(jnp.int32, (HEAD, HEAD), 1)
    inner = parity_signs(both, 7).astype(jnp.bfloat16)
    heads = stage.shape[0] // tok // len(groups)
    columns, width = heads * HEAD, heads * HEAD // chunks
    for i, group in enumerate(groups):
        there = jnp.bitwise_xor(lax.axis_index("tensor"), first + i)
        flip = (1 - 2 * bits_ref[:, pl.ds(pl.multiple_of(there * columns, HEAD), columns)]).astype(jnp.float32)
        scales = [[scale_of(ref[:, width:]) if ref.shape[1] > width else None for ref in refs] for refs in group]
        for head in range(heads):
            chunk, inside = divmod(head, heads // chunks)
            at = slice(inside * HEAD, (inside + 1) * HEAD)
            block = None
            for ref, scale in zip(group[chunk], scales[chunk]):
                term = ref[:, at] if scale is None else decode(ref[:, at], scale[:, inside : inside + 1])
                block = term if block is None else block + term
            block = block * cosine + pltpu.roll(block, HEAD // 2, 1) * sine
            stage[pl.ds((i * heads + head) * tok, tok), :] = block * flip[:, head * HEAD : (head + 1) * HEAD]
    whole = stage[...]
    high = whole.astype(jnp.bfloat16)
    rest = whole - high.astype(jnp.float32)
    mid = rest.astype(jnp.bfloat16)
    low = (rest - mid.astype(jnp.float32)).astype(jnp.bfloat16)
    dot = functools.partial(jnp.dot, preferred_element_type=jnp.float32)
    stage[...] = dot(low, inner) + dot(mid, inner) + dot(high, inner)
    for i in range(len(groups)):
        blocks = [stage[pl.ds((i * heads + head) * tok, tok), :] for head in range(heads)]
        for head, block in enumerate(butterflies(blocks)):
            stage[pl.ds((i * heads + head) * tok, tok), :] = block


def early(near, tok, *refs):
    *block_refs, cos_ref, sin_ref, bits_ref, stage = refs
    groups = [[block_refs[k::near]] for k in range(near)]
    local_part(0, 1, groups, tok, cos_ref, sin_ref, bits_ref, stage)


def final(near, chunks, tok, near_ref, *refs):
    *block_refs, cos_ref, sin_ref, bits_ref, out_ref, top_ref, stage, whole = refs
    far = len(block_refs) // chunks
    count = near + far
    groups = [[[block_refs[chunk * far + k]] for chunk in range(chunks)] for k in range(far)]
    local_part(near, chunks, groups, tok, cos_ref, sin_ref, bits_ref, stage)
    heads = stage.shape[0] // tok // far
    norm = 1.0 / float(HEAD * heads * count) ** 0.5

    def place(k, head):
        ref, k = (near_ref, k) if k < near else (stage, k - near)
        return ref[pl.ds((k * heads + head) * tok, tok), :]

    top = jnp.zeros((tok, HEAD), jnp.float32)
    for head in range(heads):
        for k, block in enumerate(butterflies([place(k, head) for k in range(count)])):
            block = block * norm
            whole[pl.ds((k * heads + head) * tok, tok), :] = block
            top = jnp.maximum(top, jnp.abs(block))
    top = jnp.max(top, axis=1, keepdims=True)
    row = lax.broadcasted_iota(jnp.int32, (tok, HEAD), 0)
    line = jnp.sum(jnp.where(row == lane_of(tok), top, 0.0), axis=0, keepdims=True)
    top_ref[...] = line[:, :tok]
    inverse = 1.0 / (top + 1e-06)
    bits = (count - 1).bit_length()
    for k in range(count):
        factor = inverse * parity_signs(jnp.bitwise_and(lax.axis_index("tensor"), k), bits)
        for head in range(heads):
            at = pl.ds((k * heads + head) * HEAD, HEAD)
            out_ref[:, at] = (whole[pl.ds((k * heads + head) * tok, tok), :] * factor).astype(jnp.bfloat16)


def swap(array, axis, count, offset):
    return lax.ppermute(array, axis, [(i, i ^ offset) for i in range(count)])


def cross(array, seqs, tensors, j, k):
    pairs = [(i, (i // seqs ^ k) * seqs + (i % seqs ^ j)) for i in range(seqs * tensors)]
    return lax.ppermute(array, ("tensor", "seq"), pairs)


def per_device(hidden_rows, kv_weight, block_lengths, sign_bits):
    tok, depth = hidden_rows.shape
    rows_dev, columns = kv_weight.shape[1:]
    which, tensor_at, seq_at = (lax.axis_index(name) for name in ("kv", "tensor", "seq"))
    cores, tensors, seqs = (lax.axis_size(name) for name in ("kv", "tensor", "seq"))
    weight = pltpu.with_memory_space_constraint(kv_weight[0], pltpu.HBM)
    part = rows_dev // cores
    vmem = pl.BlockSpec(memory_space=pltpu.VMEM)
    hbm = pl.BlockSpec(memory_space=pltpu.HBM)
    chunks = 2 if columns >= 1024 else 1
    width = columns // chunks
    near = min(2, tensors)
    order = [(j, k) for j in range(seqs) for k in range(near)]
    order += [(j, k) for j in range(seqs) for k in range(near, tensors)]

    def local(kernel, outs, in_specs, limit, scratch=(), flops=0, moved=0):
        return pl.pallas_call(
            kernel,
            in_specs=in_specs,
            out_specs=jax.tree.map(lambda _: vmem, outs),
            out_shape=outs,
            scratch_shapes=scratch,
            compiler_params=pltpu.CompilerParams(vmem_limit_bytes=limit << 20),
            cost_estimate=pl.CostEstimate(flops=flops, bytes_accessed=moved, transcendentals=0),
        )

    def loaded(weight, offset):
        return local(
            functools.partial(load, offset, 0, 8),
            pltpu.VMEM((part, columns), weight.dtype),
            [hbm],
            4,
            [pltpu.SemaphoreType.DMA((8,))],
            moved=4 * part * columns,
        )(weight)

    index = jnp.arange(block_lengths.shape[0], dtype=jnp.int32)
    starts = jnp.sum(jnp.where(index[:, None] < index[None, :], block_lengths[:, None], 0), axis=0)
    glob = (tensor_at * seqs + seq_at) * tok + jnp.arange(tok, dtype=jnp.int32)
    hits = glob[:, None] >= starts[None, :]
    place = (glob - jnp.max(jnp.where(hits, starts[None, :], 0), axis=1)).astype(jnp.float32)
    freq = jnp.float32(1000000.0) ** (-2.0 * jnp.arange(HEAD // 2, dtype=jnp.float32) / HEAD)
    angle = place[:, None] * freq[None, :]
    cosine = jnp.where(which == 0, jnp.cos(angle), 1.0)
    sine = jnp.where(which == 0, jnp.sin(angle), 0.0)
    cosine = jnp.concatenate([cosine, cosine], axis=1)
    sine = jnp.concatenate([-sine, sine], axis=1)

    slices = local(
        take,
        [pltpu.VMEM((tok, part), hidden_rows.dtype)] * seqs,
        [hbm],
        4,
        [pltpu.SemaphoreType.DMA((seqs,))],
    )(pltpu.with_memory_space_constraint(hidden_rows, pltpu.HBM))
    blocks = {(0, 0): slices[0]}
    for j in range(1, seqs):
        blocks[j, 0] = cross(slices[j], seqs, tensors, j, 0)
    for k in range(near, tensors):
        for j in range(seqs):
            blocks[j, k] = cross(slices[j], seqs, tensors, j, k)
    pair = jnp.concatenate([blocks[j, 0] for j in range(seqs)], axis=0)
    for k in range(1, near):
        got = cross(pair, seqs, tensors, 0, k)
        for j in range(seqs):
            blocks[j, k] = got[j * tok : (j + 1) * tok]
    weight, cosine, sine, blocks[1, 0] = lax.optimization_barrier((weight, cosine, sine, blocks[1, 0]))
    halves = [loaded(weight, offset) for offset in range(cores)]
    mine = jnp.concatenate([blocks[at] for at in order], axis=0)
    mine, *halves = lax.optimization_barrier((mine, *halves))
    other = swap(mine, "kv", cores, 1)
    rows = mine.shape[0]
    tile = min(256, width)
    limit = 8 if rows < 1024 else 24
    acc = local(
        functools.partial(first_half, tile),
        jax.ShapeDtypeStruct((rows, columns), jnp.float32),
        [vmem] * 2,
        limit,
        flops=2 * rows * part * columns,
        moved=4 * rows * columns,
    )(mine, halves[0])

    def second(row, count, kept, column, width, sends):
        size = (count - kept) // sends
        return local(
            functools.partial(second_half, row, count, column, tile),
            [jax.ShapeDtypeStruct((kept, width), jnp.float32)]
            + [jax.ShapeDtypeStruct((size, width + LANES), jnp.int16)] * sends,
            [vmem] * 3,
            limit,
            flops=2 * count * part * width,
            moved=8 * count * width,
        )(other, halves[1], acc)

    begin = seqs * near * tok
    away = (tensors - near) * tok
    far = []
    for chunk in range(chunks):
        keep, *sends = second(begin, rows - begin, away, chunk * width, width, seqs - 1)
        got = [cross(send, seqs, tensors, j, 0) for j, send in enumerate(sends, 1)]
        parts = local(
            functools.partial(middle, seqs),
            [jax.ShapeDtypeStruct((tok, width + LANES), jnp.int16)] * (tensors - near),
            [vmem] * seqs,
            limit,
            moved=8 * away * width,
        )(keep, *got)
        far += [cross(array, seqs, tensors, 0, k) for k, array in enumerate(parts, near)]
    keep, *sends = second(0, begin, tok, 0, columns, seqs * near - 1)
    direct = [keep] + [cross(send, seqs, tensors, *order[i]) for i, send in enumerate(sends, 1)]

    tables = cosine, sine, sign_bits[None]
    heads = columns // HEAD
    size = heads * tok * HEAD
    ready = local(
        functools.partial(early, near, tok),
        jax.ShapeDtypeStruct((near * heads * tok, HEAD), jnp.float32),
        [vmem] * (seqs * near + 3),
        16,
        flops=6 * near * size * HEAD,
        moved=8 * near * size,
    )(*direct, *tables)
    cache, top = local(
        functools.partial(final, near, chunks, tok),
        [
            jax.ShapeDtypeStruct((tok, depth), jnp.bfloat16),
            jax.ShapeDtypeStruct((1, tok), jnp.float32),
        ],
        [vmem] * ((tensors - near) * chunks + 4),
        16,
        [pltpu.VMEM((count * heads * tok, HEAD), jnp.float32) for count in (tensors - near, tensors)],
        moved=8 * tensors * size,
    )(ready, *far, *tables)
    return (cache[None], top)


def solution(mesh):
    return jax.shard_map(
        per_device,
        mesh=mesh,
        in_specs=(P(("groups", "tensor", "seq"), None), P("kv", "seq", "tensor"), P("groups"), P()),
        out_specs=(
            P("kv", ("groups", "tensor", "seq"), None),
            P("kv", ("groups", "tensor", "seq")),
        ),
        check_vma=False,
    )
```

```python
import functools

import jax
import jax.numpy as jnp
from jax import lax
from jax.experimental import pallas as pl
from jax.experimental.pallas import tpu as pltpu
from jax.sharding import PartitionSpec as P

HEAD = 128
LANES = 128
FULL = 32000.0
STEPS = 64.0
TINY = 1e-30


def encode(block):
    top = jnp.max(jnp.abs(block), axis=1, keepdims=True)
    code = jnp.ceil(jnp.log2(jnp.maximum(top, TINY)) * STEPS)
    coded = jnp.round(block * (jnp.exp2(code * (-1.0 / STEPS)) * FULL))
    return coded.astype(jnp.int32).astype(jnp.int16), code


def scale_of(codes):
    return jnp.exp2(codes.astype(jnp.int32).astype(jnp.float32) * (1.0 / STEPS)) * (1.0 / FULL)


def decode(coded, scale):
    return coded.astype(jnp.int32).astype(jnp.float32) * scale


def lane_of(rows):
    return lax.broadcasted_iota(jnp.int32, (rows, LANES), 1)


def load(offset, piece, copies, w_ref, out_ref, sems):
    rows = out_ref.shape[0]
    cores = lax.axis_size("kv")
    index = lax.rem(lax.axis_index("kv") + offset, cores)
    base = index * (w_ref.shape[0] // cores) + piece * rows
    step = rows // copies
    started = []
    for i in range(copies):
        start = pl.multiple_of(base + i * step, step)
        started.append(
            pltpu.make_async_copy(w_ref.at[pl.ds(start, step)], out_ref.at[pl.ds(i * step, step)], sems.at[i])
        )
    for copy in started:
        copy.start()
    for copy in started:
        copy.wait()


def take(rows_ref, *refs):
    out_refs, sems = refs[:-1], refs[-1]
    part = out_refs[0].shape[1]
    copies = []
    for j, out_ref in enumerate(out_refs):
        index = jnp.bitwise_xor(lax.axis_index("seq"), j) * lax.axis_size("kv") + lax.axis_index("kv")
        at = pl.ds(pl.multiple_of(index * part, part), part)
        copies.append(pltpu.make_async_copy(rows_ref.at[:, at], out_ref, sems.at[j]))
    for copy in copies:
        copy.start()
    for copy in copies:
        copy.wait()


def first_half(row, rows, tile, rows_ref, w_ref, acc_ref):
    for first in range(0, acc_ref.shape[1], tile):
        at = slice(first, first + tile)
        acc_ref[:, at] = jnp.dot(rows_ref[row : row + rows, :], w_ref[:, at], preferred_element_type=jnp.float32)


def second_half(row, rows, column, tile, rows_ref, w_ref, acc_ref, keep_ref, *send_refs):
    kept, width = keep_ref.shape
    size = send_refs[0].shape[0]
    codes = jnp.zeros((rows - kept, LANES), jnp.float32)
    lane = lane_of(rows - kept)
    for first in range(0, width, tile):
        at = slice(column + first, column + first + tile)
        total = acc_ref[row : row + rows, at]
        total = total + jnp.dot(rows_ref[row : row + rows, :], w_ref[:, at], preferred_element_type=jnp.float32)
        keep_ref[:, first : first + tile] = total[:kept]
        for begin in range(0, tile, HEAD):
            coded, code = encode(total[kept:, begin : begin + HEAD])
            head = (first + begin) // HEAD
            for i, ref in enumerate(send_refs):
                ref[:, head * HEAD : (head + 1) * HEAD] = coded[i * size : (i + 1) * size]
            codes = jnp.where(lane == head, code, codes)
    codes = codes.astype(jnp.int32).astype(jnp.int16)
    for i, ref in enumerate(send_refs):
        ref[:, width:] = codes[i * size : (i + 1) * size]


def middle(seqs, keep_ref, *refs):
    got_refs, out_refs = refs[: seqs - 1], refs[seqs - 1 :]
    rows, columns = keep_ref.shape
    tok = out_refs[0].shape[0]
    scales = [scale_of(ref[:, columns:]) for ref in got_refs]
    codes = jnp.zeros((rows, LANES), jnp.float32)
    lane = lane_of(rows)
    for head in range(columns // HEAD):
        at = slice(head * HEAD, (head + 1) * HEAD)
        total = keep_ref[:, at]
        for ref, scale in zip(got_refs, scales):
            total = total + decode(ref[:, at], scale[:, head : head + 1])
        coded, code = encode(total)
        codes = jnp.where(lane == head, code, codes)
        for k, ref in enumerate(out_refs):
            ref[:, at] = coded[k * tok : (k + 1) * tok]
    codes = codes.astype(jnp.int32).astype(jnp.int16)
    for k, ref in enumerate(out_refs):
        ref[:, columns:] = codes[k * tok : (k + 1) * tok]


def butterflies(blocks):
    blocks = list(blocks)
    span = 1
    while span < len(blocks):
        for i in range(len(blocks)):
            if not i & span:
                a, b = blocks[i], blocks[i + span]
                blocks[i], blocks[i + span] = a + b, a - b
        span *= 2
    return blocks


def parity_signs(both, bits):
    parity = jnp.zeros_like(both)
    for bit in range(bits):
        parity = parity + jnp.bitwise_and(jnp.right_shift(both, bit), 1)
    return (1 - 2 * jnp.bitwise_and(parity, 1)).astype(jnp.float32)


def local_part(first, chunks, groups, tok, cos_ref, sin_ref, bits_ref, stage):
    cosine, sine = cos_ref[...], sin_ref[...]
    both = lax.broadcasted_iota(jnp.int32, (HEAD, HEAD), 0) & lax.broadcasted_iota(jnp.int32, (HEAD, HEAD), 1)
    inner = parity_signs(both, 7).astype(jnp.bfloat16)
    heads = stage.shape[0] // tok // len(groups)
    columns, width = heads * HEAD, heads * HEAD // chunks
    for i, group in enumerate(groups):
        there = jnp.bitwise_xor(lax.axis_index("tensor"), first + i)
        flip = (1 - 2 * bits_ref[:, pl.ds(pl.multiple_of(there * columns, HEAD), columns)]).astype(jnp.float32)
        scales = [[scale_of(ref[:, width:]) if ref.shape[1] > width else None for ref in refs] for refs in group]
        for head in range(heads):
            chunk, inside = divmod(head, heads // chunks)
            at = slice(inside * HEAD, (inside + 1) * HEAD)
            block = None
            for ref, scale in zip(group[chunk], scales[chunk]):
                term = ref[:, at] if scale is None else decode(ref[:, at], scale[:, inside : inside + 1])
                block = term if block is None else block + term
            block = block * cosine + pltpu.roll(block, HEAD // 2, 1) * sine
            stage[pl.ds((i * heads + head) * tok, tok), :] = block * flip[:, head * HEAD : (head + 1) * HEAD]
    whole = stage[...]
    high = whole.astype(jnp.bfloat16)
    rest = whole - high.astype(jnp.float32)
    mid = rest.astype(jnp.bfloat16)
    low = (rest - mid.astype(jnp.float32)).astype(jnp.bfloat16)
    dot = functools.partial(jnp.dot, preferred_element_type=jnp.float32)
    stage[...] = dot(low, inner) + dot(mid, inner) + dot(high, inner)
    for i in range(len(groups)):
        blocks = [stage[pl.ds((i * heads + head) * tok, tok), :] for head in range(heads)]
        for head, block in enumerate(butterflies(blocks)):
            stage[pl.ds((i * heads + head) * tok, tok), :] = block


def early(near, tok, *refs):
    *block_refs, cos_ref, sin_ref, bits_ref, stage = refs
    groups = [[block_refs[k::near]] for k in range(near)]
    local_part(0, 1, groups, tok, cos_ref, sin_ref, bits_ref, stage)


def final(near, chunks, tok, near_ref, *refs):
    *block_refs, cos_ref, sin_ref, bits_ref, out_ref, top_ref, stage, whole = refs
    far = len(block_refs) // chunks
    count = near + far
    groups = [[[block_refs[chunk * far + k]] for chunk in range(chunks)] for k in range(far)]
    local_part(near, chunks, groups, tok, cos_ref, sin_ref, bits_ref, stage)
    heads = stage.shape[0] // tok // far
    norm = 1.0 / float(HEAD * heads * count) ** 0.5

    def place(k, head):
        ref, k = (near_ref, k) if k < near else (stage, k - near)
        return ref[pl.ds((k * heads + head) * tok, tok), :]

    top = jnp.zeros((tok, HEAD), jnp.float32)
    for head in range(heads):
        for k, block in enumerate(butterflies([place(k, head) for k in range(count)])):
            block = block * norm
            whole[pl.ds((k * heads + head) * tok, tok), :] = block
            top = jnp.maximum(top, jnp.abs(block))
    top = jnp.max(top, axis=1, keepdims=True)
    row = lax.broadcasted_iota(jnp.int32, (tok, HEAD), 0)
    line = jnp.sum(jnp.where(row == lane_of(tok), top, 0.0), axis=0, keepdims=True)
    top_ref[...] = line[:, :tok]
    inverse = 1.0 / (top + 1e-06)
    bits = (count - 1).bit_length()
    for k in range(count):
        factor = inverse * parity_signs(jnp.bitwise_and(lax.axis_index("tensor"), k), bits)
        for head in range(heads):
            at = pl.ds((k * heads + head) * HEAD, HEAD)
            out_ref[:, at] = (whole[pl.ds((k * heads + head) * tok, tok), :] * factor).astype(jnp.bfloat16)


def swap(array, axis, count, offset):
    return lax.ppermute(array, axis, [(i, i ^ offset) for i in range(count)])


def cross(array, seqs, tensors, j, k):
    pairs = [(i, (i // seqs ^ k) * seqs + (i % seqs ^ j)) for i in range(seqs * tensors)]
    return lax.ppermute(array, ("tensor", "seq"), pairs)


def per_device(hidden_rows, kv_weight, block_lengths, sign_bits):
    tok, depth = hidden_rows.shape
    rows_dev, columns = kv_weight.shape[1:]
    which, tensor_at, seq_at = (lax.axis_index(name) for name in ("kv", "tensor", "seq"))
    cores, tensors, seqs = (lax.axis_size(name) for name in ("kv", "tensor", "seq"))
    weight = pltpu.with_memory_space_constraint(kv_weight[0], pltpu.HBM)
    part = rows_dev // cores
    vmem = pl.BlockSpec(memory_space=pltpu.VMEM)
    hbm = pl.BlockSpec(memory_space=pltpu.HBM)
    chunks = 1
    near = min(2, tensors)
    order = [(j, k) for j in range(seqs) for k in range(near)]
    order += [(j, k) for j in range(seqs) for k in range(near, tensors)]

    def local(kernel, outs, in_specs, limit, scratch=(), flops=0, moved=0):
        return pl.pallas_call(
            kernel,
            in_specs=in_specs,
            out_specs=jax.tree.map(lambda _: vmem, outs),
            out_shape=outs,
            scratch_shapes=scratch,
            compiler_params=pltpu.CompilerParams(vmem_limit_bytes=limit << 20),
            cost_estimate=pl.CostEstimate(flops=flops, bytes_accessed=moved, transcendentals=0),
        )

    def loaded(weight, offset):
        return local(
            functools.partial(load, offset, 0, 8),
            pltpu.VMEM((part, columns), weight.dtype),
            [hbm],
            4,
            [pltpu.SemaphoreType.DMA((8,))],
            moved=4 * part * columns,
        )(weight)

    index = jnp.arange(block_lengths.shape[0], dtype=jnp.int32)
    starts = jnp.sum(jnp.where(index[:, None] < index[None, :], block_lengths[:, None], 0), axis=0)
    glob = (tensor_at * seqs + seq_at) * tok + jnp.arange(tok, dtype=jnp.int32)
    hits = glob[:, None] >= starts[None, :]
    place = (glob - jnp.max(jnp.where(hits, starts[None, :], 0), axis=1)).astype(jnp.float32)
    freq = jnp.float32(1000000.0) ** (-2.0 * jnp.arange(HEAD // 2, dtype=jnp.float32) / HEAD)
    angle = place[:, None] * freq[None, :]
    cosine = jnp.where(which == 0, jnp.cos(angle), 1.0)
    sine = jnp.where(which == 0, jnp.sin(angle), 0.0)
    cosine = jnp.concatenate([cosine, cosine], axis=1)
    sine = jnp.concatenate([-sine, sine], axis=1)

    slices = local(
        take,
        [pltpu.VMEM((tok, part), hidden_rows.dtype)] * seqs,
        [hbm],
        4,
        [pltpu.SemaphoreType.DMA((seqs,))],
    )(pltpu.with_memory_space_constraint(hidden_rows, pltpu.HBM))
    blocks = {(0, 0): slices[0]}
    for j in range(1, seqs):
        blocks[j, 0] = cross(slices[j], seqs, tensors, j, 0)
    for k in range(near, tensors):
        for j in range(seqs):
            blocks[j, k] = cross(slices[j], seqs, tensors, j, k)
    pair = jnp.concatenate([blocks[j, 0] for j in range(seqs)], axis=0)
    for k in range(1, near):
        got = cross(pair, seqs, tensors, 0, k)
        for j in range(seqs):
            blocks[j, k] = got[j * tok : (j + 1) * tok]
    weight, cosine, sine, blocks[1, 0] = lax.optimization_barrier((weight, cosine, sine, blocks[1, 0]))
    halves = [loaded(weight, offset) for offset in range(cores)]
    begin = seqs * near * tok
    mine = jnp.concatenate([blocks[at] for at in order], axis=0)
    mine, *halves = lax.optimization_barrier((mine, *halves))
    tile = min(256, columns)
    limit = 8 if mine.shape[0] < 1024 else 24
    wide = columns + LANES

    def projected(mine, other, row, kept, sends):
        rows = other.shape[0]
        cost = dict(flops=2 * rows * part * columns, moved=4 * rows * columns)
        acc = local(
            functools.partial(first_half, row, rows, tile),
            jax.ShapeDtypeStruct((rows, columns), jnp.float32),
            [vmem] * 2,
            limit,
            **cost,
        )(mine, halves[0])
        return local(
            functools.partial(second_half, 0, rows, 0, tile),
            [jax.ShapeDtypeStruct((kept, columns), jnp.float32)]
            + [jax.ShapeDtypeStruct(((rows - kept) // sends, wide), jnp.int16)] * sends,
            [vmem] * 3,
            limit,
            **cost,
        )(other, halves[1], acc)

    away = (tensors - near) * tok
    keep, *sends = projected(mine, swap(mine[begin:], "kv", cores, 1), begin, away, seqs - 1)
    got = [cross(send, seqs, tensors, j, 0) for j, send in enumerate(sends, 1)]
    parts = local(
        functools.partial(middle, seqs),
        [jax.ShapeDtypeStruct((tok, wide), jnp.int16)] * (tensors - near),
        [vmem] * seqs,
        limit,
        moved=8 * away * columns,
    )(keep, *got)
    far = [cross(array, seqs, tensors, 0, k) for k, array in enumerate(parts, near)]
    other = swap(mine[:begin], "kv", cores, 1)
    mine, sends = lax.optimization_barrier((mine, sends))
    keep, *sends = projected(mine, other, 0, tok, seqs * near - 1)
    direct = [keep] + [cross(send, seqs, tensors, *order[i]) for i, send in enumerate(sends, 1)]

    tables = cosine, sine, sign_bits[None]
    heads = columns // HEAD
    size = heads * tok * HEAD
    ready = local(
        functools.partial(early, near, tok),
        jax.ShapeDtypeStruct((near * heads * tok, HEAD), jnp.float32),
        [vmem] * (seqs * near + 3),
        16,
        flops=6 * near * size * HEAD,
        moved=8 * near * size,
    )(*direct, *tables)
    cache, top = local(
        functools.partial(final, near, chunks, tok),
        [
            jax.ShapeDtypeStruct((tok, depth), jnp.bfloat16),
            jax.ShapeDtypeStruct((1, tok), jnp.float32),
        ],
        [vmem] * ((tensors - near) * chunks + 4),
        16,
        [pltpu.VMEM((count * heads * tok, HEAD), jnp.float32) for count in (tensors - near, tensors)],
        moved=8 * tensors * size,
    )(ready, *far, *tables)
    return (cache[None], top)


def solution(mesh):
    return jax.shard_map(
        per_device,
        mesh=mesh,
        in_specs=(P(("groups", "tensor", "seq"), None), P("kv", "seq", "tensor"), P("groups"), P()),
        out_specs=(
            P("kv", ("groups", "tensor", "seq"), None),
            P("kv", ("groups", "tensor", "seq")),
        ),
        check_vma=False,
    )
```

```python
import functools

import jax
import jax.numpy as jnp
from jax import lax
from jax.experimental import pallas as pl
from jax.experimental.pallas import tpu as pltpu
from jax.sharding import PartitionSpec as P

HEAD = 128
LANES = 128
FULL = 32000.0
STEPS = 64.0
TINY = 1e-30


def encode(block):
    top = jnp.max(jnp.abs(block), axis=1, keepdims=True)
    code = jnp.ceil(jnp.log2(jnp.maximum(top, TINY)) * STEPS)
    coded = jnp.round(block * (jnp.exp2(code * (-1.0 / STEPS)) * FULL))
    return coded.astype(jnp.int32).astype(jnp.int16), code


def scale_of(codes):
    return jnp.exp2(codes.astype(jnp.int32).astype(jnp.float32) * (1.0 / STEPS)) * (1.0 / FULL)


def decode(coded, scale):
    return coded.astype(jnp.int32).astype(jnp.float32) * scale


def lane_of(rows):
    return lax.broadcasted_iota(jnp.int32, (rows, LANES), 1)


def load(w_ref, *refs):
    *out_refs, sems = refs
    rows = out_refs[0].shape[0]
    pieces = sems.shape[1]
    step = rows // pieces
    copies = []
    for offset, out_ref in enumerate(out_refs):
        index = lax.rem(lax.axis_index("kv") + offset, len(out_refs))
        for i in range(pieces):
            start = pl.multiple_of(index * rows + i * step, step)
            source, target = w_ref.at[pl.ds(start, step)], out_ref.at[pl.ds(i * step, step)]
            copies.append(pltpu.make_async_copy(source, target, sems.at[offset, i]))
    for copy in copies:
        copy.start()
    for copy in copies:
        copy.wait()


def take(rows_ref, *refs):
    out_refs, sems = refs[:-1], refs[-1]
    part = out_refs[0].shape[1]
    copies = []
    for j, out_ref in enumerate(out_refs):
        index = jnp.bitwise_xor(lax.axis_index("seq"), j) * lax.axis_size("kv") + lax.axis_index("kv")
        at = pl.ds(pl.multiple_of(index * part, part), part)
        copies.append(pltpu.make_async_copy(rows_ref.at[:, at], out_ref, sems.at[j]))
    for copy in copies:
        copy.start()
    for copy in copies:
        copy.wait()


def first_half(tile, rows_ref, w_ref, acc_ref):
    for first in range(0, acc_ref.shape[1], tile):
        at = slice(first, first + tile)
        acc_ref[:, at] = jnp.dot(rows_ref[...], w_ref[:, at], preferred_element_type=jnp.float32)


def second_half(keeps, tile, rows_ref, w_ref, acc_ref, *refs):
    keep_refs, send_refs = refs[:keeps], refs[keeps:]
    rows, columns = acc_ref.shape
    kept = sum(ref.shape[0] for ref in keep_refs)
    size = send_refs[0].shape[0]
    codes = jnp.zeros((rows - kept, LANES), jnp.float32)
    lane = lane_of(rows - kept)
    for first in range(0, columns, tile):
        at = slice(first, first + tile)
        total = acc_ref[:, at] + jnp.dot(rows_ref[...], w_ref[:, at], preferred_element_type=jnp.float32)
        begin = 0
        for ref in keep_refs:
            ref[:, at] = total[begin : begin + ref.shape[0]]
            begin += ref.shape[0]
        for begin in range(0, tile, HEAD):
            coded, code = encode(total[kept:, begin : begin + HEAD])
            head = (first + begin) // HEAD
            for i, ref in enumerate(send_refs):
                ref[:, head * HEAD : (head + 1) * HEAD] = coded[i * size : (i + 1) * size]
            codes = jnp.where(lane == head, code, codes)
    codes = codes.astype(jnp.int32).astype(jnp.int16)
    for i, ref in enumerate(send_refs):
        ref[:, columns:] = codes[i * size : (i + 1) * size]


def middle(seqs, keep_ref, *refs):
    got_refs, out_refs = refs[: seqs - 1], refs[seqs - 1 :]
    rows, columns = keep_ref.shape
    tok = out_refs[0].shape[0]
    scales = [scale_of(ref[:, columns:]) for ref in got_refs]
    codes = jnp.zeros((rows, LANES), jnp.float32)
    lane = lane_of(rows)
    for head in range(columns // HEAD):
        at = slice(head * HEAD, (head + 1) * HEAD)
        total = keep_ref[:, at]
        for ref, scale in zip(got_refs, scales):
            total = total + decode(ref[:, at], scale[:, head : head + 1])
        coded, code = encode(total)
        codes = jnp.where(lane == head, code, codes)
        for k, ref in enumerate(out_refs):
            ref[:, at] = coded[k * tok : (k + 1) * tok]
    codes = codes.astype(jnp.int32).astype(jnp.int16)
    for k, ref in enumerate(out_refs):
        ref[:, columns:] = codes[k * tok : (k + 1) * tok]


def butterflies(blocks):
    blocks = list(blocks)
    span = 1
    while span < len(blocks):
        for i in range(len(blocks)):
            if not i & span:
                a, b = blocks[i], blocks[i + span]
                blocks[i], blocks[i + span] = a + b, a - b
        span *= 2
    return blocks


def parity_signs(both, bits):
    parity = jnp.zeros_like(both)
    for bit in range(bits):
        parity = parity + jnp.bitwise_and(jnp.right_shift(both, bit), 1)
    return (1 - 2 * jnp.bitwise_and(parity, 1)).astype(jnp.float32)


def local_part(first, chunks, groups, tok, cos_ref, sin_ref, bits_ref, stage):
    cosine, sine = cos_ref[...], sin_ref[...]
    both = lax.broadcasted_iota(jnp.int32, (HEAD, HEAD), 0) & lax.broadcasted_iota(jnp.int32, (HEAD, HEAD), 1)
    inner = parity_signs(both, 7).astype(jnp.bfloat16)
    heads = stage.shape[0] // tok // len(groups)
    columns, width = heads * HEAD, heads * HEAD // chunks
    for i, group in enumerate(groups):
        there = jnp.bitwise_xor(lax.axis_index("tensor"), first + i)
        flip = (1 - 2 * bits_ref[:, pl.ds(pl.multiple_of(there * columns, HEAD), columns)]).astype(jnp.float32)
        scales = [[scale_of(ref[:, width:]) if ref.shape[1] > width else None for ref in refs] for refs in group]
        for head in range(heads):
            chunk, inside = divmod(head, heads // chunks)
            at = slice(inside * HEAD, (inside + 1) * HEAD)
            block = None
            for ref, scale in zip(group[chunk], scales[chunk]):
                term = ref[:, at] if scale is None else decode(ref[:, at], scale[:, inside : inside + 1])
                block = term if block is None else block + term
            block = block * cosine + pltpu.roll(block, HEAD // 2, 1) * sine
            stage[pl.ds((i * heads + head) * tok, tok), :] = block * flip[:, head * HEAD : (head + 1) * HEAD]
    whole = stage[...]
    high = whole.astype(jnp.bfloat16)
    rest = whole - high.astype(jnp.float32)
    mid = rest.astype(jnp.bfloat16)
    low = (rest - mid.astype(jnp.float32)).astype(jnp.bfloat16)
    dot = functools.partial(jnp.dot, preferred_element_type=jnp.float32)
    stage[...] = dot(low, inner) + dot(mid, inner) + dot(high, inner)
    for i in range(len(groups)):
        blocks = [stage[pl.ds((i * heads + head) * tok, tok), :] for head in range(heads)]
        for head, block in enumerate(butterflies(blocks)):
            stage[pl.ds((i * heads + head) * tok, tok), :] = block


def early(near, tok, *refs):
    *block_refs, cos_ref, sin_ref, bits_ref, stage = refs
    groups = [[block_refs[k::near]] for k in range(near)]
    local_part(0, 1, groups, tok, cos_ref, sin_ref, bits_ref, stage)


def final(near, chunks, tok, near_ref, *refs):
    *block_refs, cos_ref, sin_ref, bits_ref, out_ref, top_ref, stage, whole = refs
    far = len(block_refs) // chunks
    count = near + far
    groups = [[[block_refs[chunk * far + k]] for chunk in range(chunks)] for k in range(far)]
    local_part(near, chunks, groups, tok, cos_ref, sin_ref, bits_ref, stage)
    heads = stage.shape[0] // tok // far
    norm = 1.0 / float(HEAD * heads * count) ** 0.5

    def place(k, head):
        ref, k = (near_ref, k) if k < near else (stage, k - near)
        return ref[pl.ds((k * heads + head) * tok, tok), :]

    top = jnp.zeros((tok, HEAD), jnp.float32)
    for head in range(heads):
        for k, block in enumerate(butterflies([place(k, head) for k in range(count)])):
            block = block * norm
            whole[pl.ds((k * heads + head) * tok, tok), :] = block
            top = jnp.maximum(top, jnp.abs(block))
    top = jnp.max(top, axis=1, keepdims=True)
    row = lax.broadcasted_iota(jnp.int32, (tok, HEAD), 0)
    line = jnp.sum(jnp.where(row == lane_of(tok), top, 0.0), axis=0, keepdims=True)
    top_ref[...] = line[:, :tok]
    inverse = 1.0 / (top + 1e-06)
    bits = (count - 1).bit_length()
    for k in range(count):
        factor = inverse * parity_signs(jnp.bitwise_and(lax.axis_index("tensor"), k), bits)
        for head in range(heads):
            at = pl.ds((k * heads + head) * HEAD, HEAD)
            out_ref[:, at] = (whole[pl.ds((k * heads + head) * tok, tok), :] * factor).astype(jnp.bfloat16)


def swap(array, axis, count, offset):
    return lax.ppermute(array, axis, [(i, i ^ offset) for i in range(count)])


def cross(array, seqs, tensors, j, k):
    pairs = [(i, (i // seqs ^ k) * seqs + (i % seqs ^ j)) for i in range(seqs * tensors)]
    return lax.ppermute(array, ("tensor", "seq"), pairs)


def per_device(hidden_rows, kv_weight, block_lengths, sign_bits):
    tok, depth = hidden_rows.shape
    rows_dev, columns = kv_weight.shape[1:]
    which, tensor_at, seq_at = (lax.axis_index(name) for name in ("kv", "tensor", "seq"))
    cores, tensors, seqs = (lax.axis_size(name) for name in ("kv", "tensor", "seq"))
    weight = pltpu.with_memory_space_constraint(kv_weight[0], pltpu.HBM)
    part = rows_dev // cores
    vmem = pl.BlockSpec(memory_space=pltpu.VMEM)
    hbm = pl.BlockSpec(memory_space=pltpu.HBM)
    chunks = 1
    near = min(2, tensors)

    def local(kernel, outs, in_specs, limit, scratch=(), flops=0, moved=0):
        return pl.pallas_call(
            kernel,
            in_specs=in_specs,
            out_specs=jax.tree.map(lambda _: vmem, outs),
            out_shape=outs,
            scratch_shapes=scratch,
            compiler_params=pltpu.CompilerParams(vmem_limit_bytes=limit << 20),
            cost_estimate=pl.CostEstimate(flops=flops, bytes_accessed=moved, transcendentals=0),
        )

    def loaded(weight):
        return local(
            load,
            [pltpu.VMEM((part, columns), weight.dtype)] * cores,
            [hbm],
            4,
            [pltpu.SemaphoreType.DMA((cores, 8))],
            moved=4 * rows_dev * columns,
        )(weight)

    index = jnp.arange(block_lengths.shape[0], dtype=jnp.int32)
    starts = jnp.sum(jnp.where(index[:, None] < index[None, :], block_lengths[:, None], 0), axis=0)
    glob = (tensor_at * seqs + seq_at) * tok + jnp.arange(tok, dtype=jnp.int32)
    hits = glob[:, None] >= starts[None, :]
    place = (glob - jnp.max(jnp.where(hits, starts[None, :], 0), axis=1)).astype(jnp.float32)
    freq = jnp.float32(1000000.0) ** (-2.0 * jnp.arange(HEAD // 2, dtype=jnp.float32) / HEAD)
    angle = place[:, None] * freq[None, :]
    cosine = jnp.where(which == 0, jnp.cos(angle), 1.0)
    sine = jnp.where(which == 0, jnp.sin(angle), 0.0)
    cosine = jnp.concatenate([cosine, cosine], axis=1)
    sine = jnp.concatenate([-sine, sine], axis=1)

    slices = local(
        take,
        [pltpu.VMEM((tok, part), hidden_rows.dtype)] * seqs,
        [hbm],
        4,
        [pltpu.SemaphoreType.DMA((seqs,))],
    )(pltpu.with_memory_space_constraint(hidden_rows, pltpu.HBM))
    blocks = {(0, 0): slices[0]}
    for j in range(1, seqs):
        blocks[j, 0] = cross(slices[j], seqs, tensors, j, 0)
        for k in range(near, tensors):
            blocks[j, k] = cross(slices[j], seqs, tensors, j, k)
    own = slices[0]
    for k in range(near, tensors):
        blocks[0, k] = cross(own, seqs, tensors, 0, k)
    pair = jnp.concatenate([blocks[j, 0] for j in range(seqs)], axis=0)
    for k in range(1, near):
        got = cross(pair, seqs, tensors, 0, k)
        for j in range(seqs):
            blocks[j, k] = got[j * tok : (j + 1) * tok]
    remote = jnp.concatenate([blocks[j, k] for j in range(1, seqs) for k in range(near, tensors)], axis=0)
    order = [(0, k) for k in range(near, tensors)] + [(j, k) for j in range(seqs) for k in range(near)]
    weight, cosine, sine, blocks[1, 0] = lax.optimization_barrier((weight, cosine, sine, blocks[1, 0]))
    halves = loaded(weight)
    remote, *halves = lax.optimization_barrier((remote, *halves))
    tile = min(256, columns)
    limit = 8 if remote.shape[0] < 1024 else 24
    wide = columns + LANES

    def projected(mine, other, keeps, sends):
        rows = mine.shape[0]
        size = (rows - sum(keeps)) // sends
        cost = dict(flops=2 * rows * part * columns, moved=4 * rows * columns)
        acc = local(
            functools.partial(first_half, tile),
            jax.ShapeDtypeStruct((rows, columns), jnp.float32),
            [vmem] * 2,
            limit,
            **cost,
        )(mine, halves[0])
        outs = local(
            functools.partial(second_half, len(keeps), tile),
            [jax.ShapeDtypeStruct((keep, columns), jnp.float32) for keep in keeps]
            + [jax.ShapeDtypeStruct((size, wide), jnp.int16)] * sends,
            [vmem] * 3,
            limit,
            **cost,
        )(other, halves[1], acc)
        return outs[: len(keeps)], outs[len(keeps) :]

    away = (tensors - near) * tok
    _, sends = projected(remote, swap(remote, "kv", cores, 1), [], seqs - 1)
    got = [cross(send, seqs, tensors, j, 0) for j, send in enumerate(sends, 1)]
    late, sends = lax.optimization_barrier(([blocks[at] for at in order], sends))
    mine = jnp.concatenate(late, axis=0)
    other = swap(mine, "kv", cores, 1)
    (keep, first), sends = projected(mine, other, [away, tok], seqs * near - 1)
    parts = local(
        functools.partial(middle, seqs),
        [jax.ShapeDtypeStruct((tok, wide), jnp.int16)] * (tensors - near),
        [vmem] * seqs,
        limit,
        moved=8 * away * columns,
    )(keep, *got)
    far = [cross(array, seqs, tensors, 0, k) for k, array in enumerate(parts, near)]
    close = [(j, k) for j in range(seqs) for k in range(near)]
    direct = [first] + [cross(send, seqs, tensors, *close[i]) for i, send in enumerate(sends, 1)]

    tables = cosine, sine, sign_bits[None]
    heads = columns // HEAD
    size = heads * tok * HEAD
    ready = local(
        functools.partial(early, near, tok),
        jax.ShapeDtypeStruct((near * heads * tok, HEAD), jnp.float32),
        [vmem] * (seqs * near + 3),
        16,
        flops=6 * near * size * HEAD,
        moved=8 * near * size,
    )(*direct, *tables)
    cache, top = local(
        functools.partial(final, near, chunks, tok),
        [
            jax.ShapeDtypeStruct((tok, depth), jnp.bfloat16),
            jax.ShapeDtypeStruct((1, tok), jnp.float32),
        ],
        [vmem] * ((tensors - near) * chunks + 4),
        16,
        [pltpu.VMEM((count * heads * tok, HEAD), jnp.float32) for count in (tensors - near, tensors)],
        moved=8 * tensors * size,
    )(ready, *far, *tables)
    return (cache[None], top)


def solution(mesh):
    return jax.shard_map(
        per_device,
        mesh=mesh,
        in_specs=(P(("groups", "tensor", "seq"), None), P("kv", "seq", "tensor"), P("groups"), P()),
        out_specs=(
            P("kv", ("groups", "tensor", "seq"), None),
            P("kv", ("groups", "tensor", "seq")),
        ),
        check_vma=False,
    )
```

```python
import functools

import jax
import jax.numpy as jnp
from jax import lax
from jax.experimental import pallas as pl
from jax.experimental.pallas import tpu as pltpu
from jax.sharding import PartitionSpec as P

HEAD = 128
LANES = 128
FULL = 32000.0
STEPS = 64.0
TINY = 1e-30


def encode(block):
    top = jnp.max(jnp.abs(block), axis=1, keepdims=True)
    code = jnp.ceil(jnp.log2(jnp.maximum(top, TINY)) * STEPS)
    coded = jnp.round(block * (jnp.exp2(code * (-1.0 / STEPS)) * FULL))
    return coded.astype(jnp.int32).astype(jnp.int16), code


def scale_of(codes):
    return jnp.exp2(codes.astype(jnp.int32).astype(jnp.float32) * (1.0 / STEPS)) * (1.0 / FULL)


def decode(coded, scale):
    return coded.astype(jnp.int32).astype(jnp.float32) * scale


def lane_of(rows):
    return lax.broadcasted_iota(jnp.int32, (rows, LANES), 1)


def load(w_ref, *refs):
    *out_refs, sems = refs
    rows = out_refs[0].shape[0]
    pieces = sems.shape[1]
    step = rows // pieces
    copies = []
    for offset, out_ref in enumerate(out_refs):
        index = lax.rem(lax.axis_index("kv") + offset, len(out_refs))
        for i in range(pieces):
            start = pl.multiple_of(index * rows + i * step, step)
            source, target = w_ref.at[pl.ds(start, step)], out_ref.at[pl.ds(i * step, step)]
            copies.append(pltpu.make_async_copy(source, target, sems.at[offset, i]))
    for copy in copies:
        copy.start()
    for copy in copies:
        copy.wait()


def take(rows_ref, *refs):
    out_refs, sems = refs[:-1], refs[-1]
    part = out_refs[0].shape[1]
    copies = []
    for j, out_ref in enumerate(out_refs):
        index = jnp.bitwise_xor(lax.axis_index("seq"), j) * lax.axis_size("kv") + lax.axis_index("kv")
        at = pl.ds(pl.multiple_of(index * part, part), part)
        copies.append(pltpu.make_async_copy(rows_ref.at[:, at], out_ref, sems.at[j]))
    for copy in copies:
        copy.start()
    for copy in copies:
        copy.wait()


def first_half(tile, rows_ref, w_ref, acc_ref):
    for first in range(0, acc_ref.shape[1], tile):
        at = slice(first, first + tile)
        acc_ref[:, at] = jnp.dot(rows_ref[...], w_ref[:, at], preferred_element_type=jnp.float32)


def second_half(keeps, tile, rows_ref, w_ref, acc_ref, *refs):
    keep_refs, send_refs = refs[:keeps], refs[keeps:]
    rows, columns = acc_ref.shape
    kept = sum(ref.shape[0] for ref in keep_refs)
    size = send_refs[0].shape[0]
    codes = jnp.zeros((rows - kept, LANES), jnp.float32)
    lane = lane_of(rows - kept)
    for first in range(0, columns, tile):
        at = slice(first, first + tile)
        total = acc_ref[:, at] + jnp.dot(rows_ref[...], w_ref[:, at], preferred_element_type=jnp.float32)
        begin = 0
        for ref in keep_refs:
            ref[:, at] = total[begin : begin + ref.shape[0]]
            begin += ref.shape[0]
        for begin in range(0, tile, HEAD):
            coded, code = encode(total[kept:, begin : begin + HEAD])
            head = (first + begin) // HEAD
            for i, ref in enumerate(send_refs):
                ref[:, head * HEAD : (head + 1) * HEAD] = coded[i * size : (i + 1) * size]
            codes = jnp.where(lane == head, code, codes)
    codes = codes.astype(jnp.int32).astype(jnp.int16)
    for i, ref in enumerate(send_refs):
        ref[:, columns:] = codes[i * size : (i + 1) * size]


def middle(seqs, keep_ref, *refs):
    got_refs, out_refs = refs[: seqs - 1], refs[seqs - 1 :]
    rows, columns = keep_ref.shape
    tok = out_refs[0].shape[0]
    scales = [scale_of(ref[:, columns:]) for ref in got_refs]
    codes = jnp.zeros((rows, LANES), jnp.float32)
    lane = lane_of(rows)
    heads = range(columns // HEAD)
    spans = [slice(head * HEAD, (head + 1) * HEAD) for head in heads]
    totals = []
    for head, at in zip(heads, spans):
        total = keep_ref[:, at]
        for ref, scale in zip(got_refs, scales):
            total = total + decode(ref[:, at], scale[:, head : head + 1])
        totals.append(total)
    pairs = [encode(total) for total in totals]
    for head, (_, code) in zip(heads, pairs):
        codes = jnp.where(lane == head, code, codes)
    for at, (coded, _) in zip(spans, pairs):
        for k, ref in enumerate(out_refs):
            ref[:, at] = coded[k * tok : (k + 1) * tok]
    codes = codes.astype(jnp.int32).astype(jnp.int16)
    for k, ref in enumerate(out_refs):
        ref[:, columns:] = codes[k * tok : (k + 1) * tok]


def butterflies(blocks):
    blocks = list(blocks)
    span = 1
    while span < len(blocks):
        for i in range(len(blocks)):
            if not i & span:
                a, b = blocks[i], blocks[i + span]
                blocks[i], blocks[i + span] = a + b, a - b
        span *= 2
    return blocks


def parity_signs(both, bits):
    parity = jnp.zeros_like(both)
    for bit in range(bits):
        parity = parity + jnp.bitwise_and(jnp.right_shift(both, bit), 1)
    return (1 - 2 * jnp.bitwise_and(parity, 1)).astype(jnp.float32)


def local_part(first, chunks, groups, tok, cos_ref, sin_ref, bits_ref, stage):
    cosine, sine = cos_ref[...], sin_ref[...]
    both = lax.broadcasted_iota(jnp.int32, (HEAD, HEAD), 0) & lax.broadcasted_iota(jnp.int32, (HEAD, HEAD), 1)
    inner = parity_signs(both, 7).astype(jnp.bfloat16)
    heads = stage.shape[0] // tok // len(groups)
    columns, width = heads * HEAD, heads * HEAD // chunks
    for i, group in enumerate(groups):
        there = jnp.bitwise_xor(lax.axis_index("tensor"), first + i)
        flip = (1 - 2 * bits_ref[:, pl.ds(pl.multiple_of(there * columns, HEAD), columns)]).astype(jnp.float32)
        scales = [[scale_of(ref[:, width:]) if ref.shape[1] > width else None for ref in refs] for refs in group]
        for head in range(heads):
            chunk, inside = divmod(head, heads // chunks)
            at = slice(inside * HEAD, (inside + 1) * HEAD)
            block = None
            for ref, scale in zip(group[chunk], scales[chunk]):
                term = ref[:, at] if scale is None else decode(ref[:, at], scale[:, inside : inside + 1])
                block = term if block is None else block + term
            block = block * cosine + pltpu.roll(block, HEAD // 2, 1) * sine
            stage[pl.ds((i * heads + head) * tok, tok), :] = block * flip[:, head * HEAD : (head + 1) * HEAD]
    whole = stage[...]
    high = whole.astype(jnp.bfloat16)
    rest = whole - high.astype(jnp.float32)
    mid = rest.astype(jnp.bfloat16)
    low = (rest - mid.astype(jnp.float32)).astype(jnp.bfloat16)
    dot = functools.partial(jnp.dot, preferred_element_type=jnp.float32)
    stage[...] = dot(low, inner) + dot(mid, inner) + dot(high, inner)
    for i in range(len(groups)):
        blocks = [stage[pl.ds((i * heads + head) * tok, tok), :] for head in range(heads)]
        for head, block in enumerate(butterflies(blocks)):
            stage[pl.ds((i * heads + head) * tok, tok), :] = block


def early(near, tok, *refs):
    *block_refs, cos_ref, sin_ref, bits_ref, stage = refs
    groups = [[block_refs[k::near]] for k in range(near)]
    local_part(0, 1, groups, tok, cos_ref, sin_ref, bits_ref, stage)


def final(near, chunks, tok, near_ref, *refs):
    *block_refs, cos_ref, sin_ref, bits_ref, out_ref, top_ref, stage, whole = refs
    far = len(block_refs) // chunks
    count = near + far
    groups = [[[block_refs[chunk * far + k]] for chunk in range(chunks)] for k in range(far)]
    local_part(near, chunks, groups, tok, cos_ref, sin_ref, bits_ref, stage)
    heads = stage.shape[0] // tok // far
    norm = 1.0 / float(HEAD * heads * count) ** 0.5

    def place(k, head):
        ref, k = (near_ref, k) if k < near else (stage, k - near)
        return ref[pl.ds((k * heads + head) * tok, tok), :]

    top = jnp.zeros((tok, HEAD), jnp.float32)
    for head in range(heads):
        for k, block in enumerate(butterflies([place(k, head) for k in range(count)])):
            block = block * norm
            whole[pl.ds((k * heads + head) * tok, tok), :] = block
            top = jnp.maximum(top, jnp.abs(block))
    top = jnp.max(top, axis=1, keepdims=True)
    row = lax.broadcasted_iota(jnp.int32, (tok, HEAD), 0)
    line = jnp.sum(jnp.where(row == lane_of(tok), top, 0.0), axis=0, keepdims=True)
    top_ref[...] = line[:, :tok]
    inverse = 1.0 / (top + 1e-06)
    bits = (count - 1).bit_length()
    for k in range(count):
        factor = inverse * parity_signs(jnp.bitwise_and(lax.axis_index("tensor"), k), bits)
        for head in range(heads):
            at = pl.ds((k * heads + head) * HEAD, HEAD)
            out_ref[:, at] = (whole[pl.ds((k * heads + head) * tok, tok), :] * factor).astype(jnp.bfloat16)


def swap(array, axis, count, offset):
    return lax.ppermute(array, axis, [(i, i ^ offset) for i in range(count)])


def cross(array, seqs, tensors, j, k):
    pairs = [(i, (i // seqs ^ k) * seqs + (i % seqs ^ j)) for i in range(seqs * tensors)]
    return lax.ppermute(array, ("tensor", "seq"), pairs)


def per_device(hidden_rows, kv_weight, block_lengths, sign_bits):
    tok, depth = hidden_rows.shape
    rows_dev, columns = kv_weight.shape[1:]
    which, tensor_at, seq_at = (lax.axis_index(name) for name in ("kv", "tensor", "seq"))
    cores, tensors, seqs = (lax.axis_size(name) for name in ("kv", "tensor", "seq"))
    weight = pltpu.with_memory_space_constraint(kv_weight[0], pltpu.HBM)
    part = rows_dev // cores
    vmem = pl.BlockSpec(memory_space=pltpu.VMEM)
    hbm = pl.BlockSpec(memory_space=pltpu.HBM)
    chunks = 1
    near = min(2, tensors)

    def local(kernel, outs, in_specs, limit, scratch=(), flops=0, moved=0):
        return pl.pallas_call(
            kernel,
            in_specs=in_specs,
            out_specs=jax.tree.map(lambda _: vmem, outs),
            out_shape=outs,
            scratch_shapes=scratch,
            compiler_params=pltpu.CompilerParams(vmem_limit_bytes=limit << 20),
            cost_estimate=pl.CostEstimate(flops=flops, bytes_accessed=moved, transcendentals=0),
        )

    def loaded(weight):
        return local(
            load,
            [pltpu.VMEM((part, columns), weight.dtype)] * cores,
            [hbm],
            4,
            [pltpu.SemaphoreType.DMA((cores, 8))],
            moved=4 * rows_dev * columns,
        )(weight)

    index = jnp.arange(block_lengths.shape[0], dtype=jnp.int32)
    starts = jnp.sum(jnp.where(index[:, None] < index[None, :], block_lengths[:, None], 0), axis=0)
    glob = (tensor_at * seqs + seq_at) * tok + jnp.arange(tok, dtype=jnp.int32)
    hits = glob[:, None] >= starts[None, :]
    place = (glob - jnp.max(jnp.where(hits, starts[None, :], 0), axis=1)).astype(jnp.float32)
    freq = jnp.float32(1000000.0) ** (-2.0 * jnp.arange(HEAD // 2, dtype=jnp.float32) / HEAD)
    angle = place[:, None] * freq[None, :]
    cosine = jnp.where(which == 0, jnp.cos(angle), 1.0)
    sine = jnp.where(which == 0, jnp.sin(angle), 0.0)
    cosine = jnp.concatenate([cosine, cosine], axis=1)
    sine = jnp.concatenate([-sine, sine], axis=1)

    slices = local(
        take,
        [pltpu.VMEM((tok, part), hidden_rows.dtype)] * seqs,
        [hbm],
        4,
        [pltpu.SemaphoreType.DMA((seqs,))],
    )(pltpu.with_memory_space_constraint(hidden_rows, pltpu.HBM))
    blocks = {(0, 0): slices[0]}
    for j in range(1, seqs):
        blocks[j, 0] = cross(slices[j], seqs, tensors, j, 0)
        for k in range(near, tensors):
            blocks[j, k] = cross(slices[j], seqs, tensors, j, k)
    own = slices[0]
    for k in range(near, tensors):
        blocks[0, k] = cross(own, seqs, tensors, 0, k)
    pair = jnp.concatenate([blocks[j, 0] for j in range(seqs)], axis=0)
    for k in range(1, near):
        got = cross(pair, seqs, tensors, 0, k)
        for j in range(seqs):
            blocks[j, k] = got[j * tok : (j + 1) * tok]
    remote = jnp.concatenate([blocks[j, k] for j in range(1, seqs) for k in range(near, tensors)], axis=0)
    order = [(0, k) for k in range(near, tensors)] + [(j, k) for j in range(seqs) for k in range(near)]
    weight, cosine, sine, blocks[1, 0] = lax.optimization_barrier((weight, cosine, sine, blocks[1, 0]))
    halves = loaded(weight)
    remote, *halves = lax.optimization_barrier((remote, *halves))
    tile = min(256, columns)
    limit = 8 if remote.shape[0] < 1024 else 24
    wide = columns + LANES

    def projected(mine, other, keeps, sends):
        rows = mine.shape[0]
        size = (rows - sum(keeps)) // sends
        cost = dict(flops=2 * rows * part * columns, moved=4 * rows * columns)
        acc = local(
            functools.partial(first_half, tile),
            jax.ShapeDtypeStruct((rows, columns), jnp.float32),
            [vmem] * 2,
            limit,
            **cost,
        )(mine, halves[0])
        outs = local(
            functools.partial(second_half, len(keeps), tile),
            [jax.ShapeDtypeStruct((keep, columns), jnp.float32) for keep in keeps]
            + [jax.ShapeDtypeStruct((size, wide), jnp.int16)] * sends,
            [vmem] * 3,
            limit,
            **cost,
        )(other, halves[1], acc)
        return outs[: len(keeps)], outs[len(keeps) :]

    away = (tensors - near) * tok
    _, sends = projected(remote, swap(remote, "kv", cores, 1), [], seqs - 1)
    got = [cross(send, seqs, tensors, j, 0) for j, send in enumerate(sends, 1)]
    late, sends = lax.optimization_barrier(([blocks[at] for at in order], sends))
    mine = jnp.concatenate(late, axis=0)
    other = swap(mine, "kv", cores, 1)
    (keep, first), sends = projected(mine, other, [away, tok], seqs * near - 1)
    parts = local(
        functools.partial(middle, seqs),
        [jax.ShapeDtypeStruct((tok, wide), jnp.int16)] * (tensors - near),
        [vmem] * seqs,
        limit,
        moved=8 * away * columns,
    )(keep, *got)
    far = [cross(array, seqs, tensors, 0, k) for k, array in enumerate(parts, near)]
    close = [(j, k) for j in range(seqs) for k in range(near)]
    direct = [first] + [cross(send, seqs, tensors, *close[i]) for i, send in enumerate(sends, 1)]

    tables = cosine, sine, sign_bits[None]
    heads = columns // HEAD
    size = heads * tok * HEAD
    ready = local(
        functools.partial(early, near, tok),
        jax.ShapeDtypeStruct((near * heads * tok, HEAD), jnp.float32),
        [vmem] * (seqs * near + 3),
        16,
        flops=6 * near * size * HEAD,
        moved=8 * near * size,
    )(*direct, *tables)
    cache, top = local(
        functools.partial(final, near, chunks, tok),
        [
            jax.ShapeDtypeStruct((tok, depth), jnp.bfloat16),
            jax.ShapeDtypeStruct((1, tok), jnp.float32),
        ],
        [vmem] * ((tensors - near) * chunks + 4),
        16,
        [pltpu.VMEM((count * heads * tok, HEAD), jnp.float32) for count in (tensors - near, tensors)],
        moved=8 * tensors * size,
    )(ready, *far, *tables)
    return (cache[None], top)


def solution(mesh):
    return jax.shard_map(
        per_device,
        mesh=mesh,
        in_specs=(P(("groups", "tensor", "seq"), None), P("kv", "seq", "tensor"), P("groups"), P()),
        out_specs=(
            P("kv", ("groups", "tensor", "seq"), None),
            P("kv", ("groups", "tensor", "seq")),
        ),
        check_vma=False,
    )
```
